128 devices in a mesh: tiles: 32 (over x, z, core), swath: 4 (over y).
Axes of the slice: x: 4, y: 4, z: 4, core: 2. Of those that a mesh axis runs over, the one named last changes fastest.
Arguments:
- blk_temp: bfloat16 [1536, 128, 512], P(('tiles', 'swath')), may hold values from -6 to 6
- blk_qual: bfloat16 [1536, 128, 512], P(('tiles', 'swath')), may hold values from 0.25 to 4
- dest_tile: int32 [1536], P(('tiles', 'swath')), may hold values from 0 to 31, as said below
- blk_offset: int32 [1536], P(('tiles', 'swath')), may hold values from 0 to 384
- background: float32 [16384, 512], P('tiles', 'swath'), may hold values from -6 to 6
- reflect: bfloat16 [6, 16384, 512], P(None, 'tiles', 'swath'), may hold values from -6 to 6
- land: int32 [16384, 512], P('tiles', 'swath'), may hold values 0 or 1
- conv_first: bfloat16 [16, 16, 3, 3], replicated, may hold values from -0.75 to 0.75
- bias_first: float32 [16], replicated, may hold values from -3 to 3
- conv_second: bfloat16 [16, 16, 3, 3], replicated, may hold values from -0.75 to 0.75
- bias_second: float32 [16], replicated, may hold values from -3 to 3
- conv_third: bfloat16 [16, 16, 3, 3], replicated, may hold values from -0.75 to 0.75
- bias_third: float32 [16], replicated, may hold values from -3 to 3
- head: bfloat16 [16], replicated, may hold values from -2 to 2
Outputs:
- sharp_temp: float32 [16384, 512], P('tiles', 'swath')
- fit_coefs: float32 [7], replicated
The draws below stay inside these ranges and needn't reach their ends.
Inputs may be any that keep to these rules, and one draw needn't show every extreme that they name: `dest_tile`: at most 2 of the blocks of one device have destination tile i, for each index i of tiles; one index of tiles receives exactly 2 blocks from every device.
All inputs are finite; a program needn't handle non-finite values. No bound on the sum of `land` on one device may be relied on, other than what follows from the above.
Results may differ from the reference program's by a relative error of at most 0.0072.
Values may be sent and summed in bfloat16 or wider, within the bound.
No kernel may reach another device: no remote copies, remote signals or barrier semaphores. Data moves between devices by JAX's collectives and lax.ppermute only.
A program may use at most 192 MiB of HBM per device.

```python
import math
import jax
import jax.numpy as jnp
from jax import lax

TR = 512
TC = 512
BR = 128
RADIUS = 7
NBANDS = 6
CH = 16
TILE_DEV = 1
NB_DEV = 12
CAP = 2
NT = 32
NR = 16384
NBLK = 1536
N_TILES = 32
DEVICES = 128


def draw_dest_tile(key, part):
    key_hot = jax.random.fold_in(key, 11)
    key_slot = jax.random.fold_in(key, 12)
    key_place = jax.random.fold_in(key, 13)
    key_tile = jax.random.fold_in(key, 14)
    slot_total = N_TILES * CAP
    hot_owner = jax.random.randint(key_hot, (), 0, N_TILES)
    position = jnp.arange(slot_total, dtype=jnp.int32)
    scores = jax.random.randint(key_slot, (DEVICES, slot_total), 0, 2 ** 20) * slot_total + position[None, :]
    scores = jnp.where((position // CAP == hot_owner)[None, :], position[None, :] - slot_total, scores)
    ordering = jnp.argsort(scores, axis=1)
    chosen = ordering[:, :NB_DEV]
    places = jax.random.randint(key_place, (DEVICES, NB_DEV), 0, 2 ** 20) * NB_DEV + jnp.arange(NB_DEV, dtype=jnp.int32)[None, :]
    shuffle = jnp.argsort(places, axis=1)
    chosen = jnp.take_along_axis(chosen, shuffle, axis=1)
    owner_ids = chosen // CAP
    tile_pick = jax.random.randint(key_tile, (DEVICES, NB_DEV), 0, TILE_DEV)
    return (owner_ids * TILE_DEV + tile_pick).reshape(NB_DEV * DEVICES).astype(jnp.int32)


def with_ends(array, stream_key, least, top_value):
    index_at = [jax.random.randint(jax.random.fold_in(stream_key, axis), (), 0, length) for axis, length in enumerate(array.shape)]
    main_axis = array.shape.index(max(array.shape))
    neighbour = index_at[:main_axis] + [(index_at[main_axis] + 1) % array.shape[main_axis]] + index_at[main_axis + 1:]
    return array.at[tuple(index_at)].set(least).at[tuple(neighbour)].set(top_value)


def level_of(own_key, dims, cuts, low, largest):
    factor_of, own = 1.0, jax.random.fold_in(own_key, 6)
    for dim, shards_of in cuts:
        steps = jnp.exp(jax.random.uniform(jax.random.fold_in(own, dim), (shards_of,), jnp.float32, low / len(cuts), largest / len(cuts)))
        factor_of = factor_of * jnp.repeat(steps, dims[dim] // shards_of).reshape([-1 if axis == dim else 1 for axis in range(len(dims))])
    return factor_of


def gaussian(stream_key, extent, deviation, most, cuts=(), kind=jnp.bfloat16):
    gain = level_of(stream_key, extent, cuts, -0.22, 0.18) if cuts else 1.0
    values = jax.random.normal(stream_key, extent, jnp.float32) * deviation * gain
    return jnp.minimum(jnp.maximum(values, -most), most).astype(kind)


def setup_inputs(seed: int = 0) -> dict:
    seeds = jax.random.split(jax.random.key(seed), 15)
    blk_temp = gaussian(seeds[0], (NBLK, BR, TC), 1.0, 6.0, ((0, 128),))
    blk_qual = jnp.clip(jnp.exp(math.log(4.0) - 2.7725887 * jax.random.uniform(seeds[1], (NBLK, BR, TC), jnp.float32) ** level_of(seeds[1], (NBLK, BR, TC), ((0, 128),), -0.2, 0.2)), 0.25, 4.0).astype(jnp.bfloat16)
    dest_tile = draw_dest_tile(jax.random.fold_in(seeds[14], 71), 0)
    blk_offset = with_ends(jax.random.randint(seeds[3], (NBLK,), 0, TR - BR + 1), jax.random.fold_in(seeds[3], 1), 0, TR - BR).astype(jnp.int32)
    background = gaussian(seeds[4], (NR, TC), 1.0, 6.0, ((0, 32), (1, 4)), jnp.float32)
    reflect = gaussian(seeds[5], (NBANDS, NR, TC), 1.0, 6.0, ((1, 32), (2, 4)))
    land = with_ends((jax.random.randint(seeds[6], (NR, TC), 0, 4) < 3).astype(jnp.int32), jax.random.fold_in(seeds[6], 1), 0, 1)
    conv_first = gaussian(seeds[7], (CH, CH, 3, 3), (9 * CH // 2) ** -0.5, 0.75)
    bias_first = gaussian(seeds[8], (CH,), 0.5, 3.0, (), jnp.float32)
    conv_second = gaussian(seeds[9], (CH, CH, 3, 3), (9 * CH // 2) ** -0.5, 0.75)
    bias_second = gaussian(seeds[10], (CH,), 0.5, 3.0, (), jnp.float32)
    conv_third = gaussian(seeds[11], (CH, CH, 3, 3), (9 * CH // 2) ** -0.5, 0.75)
    bias_third = gaussian(seeds[12], (CH,), 0.5, 3.0, (), jnp.float32)
    head = gaussian(seeds[13], (CH,), (CH // 2) ** -0.5, 2.0)
    return dict(blk_temp=blk_temp, blk_qual=blk_qual, dest_tile=dest_tile, blk_offset=blk_offset, background=background, reflect=reflect, land=land, conv_first=conv_first, bias_first=bias_first, conv_second=conv_second, bias_second=bias_second, conv_third=conv_third, bias_third=bias_third, head=head)


prior_weight = 0.5
ridge_term = 1.0
highest = lax.Precision.HIGHEST


def gauss_taps():
    offsets = jnp.arange(2 * RADIUS + 1, dtype=jnp.float32) - RADIUS
    raw_taps = jnp.exp(-0.125 * offsets * offsets)
    return raw_taps / jnp.sum(raw_taps)


def blur(field, weights):
    full_span = 2 * RADIUS
    height = field.shape[1] - full_span
    width = field.shape[2] - full_span
    across = weights[0] * field[:, 0:height, :]
    for tap_index in range(1, full_span + 1):
        across = across + weights[tap_index] * field[:, tap_index:tap_index + height, :]
    result = weights[0] * across[:, :, 0:width]
    for tap_index in range(1, full_span + 1):
        result = result + weights[tap_index] * across[:, :, tap_index:tap_index + width]
    return result


def solve_small(matrix, vector):
    dimension = matrix.shape[0]
    working = matrix
    solution = vector
    for pivot_index in range(dimension):
        scale_row = working[pivot_index] / working[pivot_index, pivot_index]
        scale_val = solution[pivot_index] / working[pivot_index, pivot_index]
        factor = working[:, pivot_index]
        working = working - factor[:, None] * scale_row[None, :]
        solution = solution - factor * scale_val
        working = working.at[pivot_index].set(scale_row)
        solution = solution.at[pivot_index].set(scale_val)
    return solution


def fit(smooth, land_frac):
    feature_count = smooth.shape[0]
    cell_count = smooth.shape[1] * smooth.shape[2]
    columns = jnp.concatenate([jnp.ones((1, cell_count), smooth.dtype), smooth[1:].reshape(feature_count - 1, cell_count)], axis=0)
    target = smooth[0].reshape(cell_count)
    masked = columns * land_frac.reshape(1, cell_count)
    normal = lax.dot_general(masked, columns, (((1,), (1,)), ((), ())), precision=highest)
    right_side = jnp.dot(masked, target, precision=highest)
    return normal, right_side


def build_stack(raw_fields, smooth, land_frac, fit_coefs):
    detail = jnp.tensordot(fit_coefs[1:], raw_fields[1:] - smooth[1:], axes=1, precision=highest)
    base_field = smooth[0] + detail
    stacked = jnp.concatenate([base_field[None], raw_fields[0:1], smooth[0:1], land_frac[None], raw_fields[1:], smooth[1:]], axis=0)
    return base_field, stacked


def convolve(field, kernel, bias_term):
    out_field = lax.conv_general_dilated(field.astype(jnp.float32)[None], kernel.astype(jnp.float32), (1, 1), "VALID", dimension_numbers=("NCHW", "OIHW", "NCHW"), precision=highest)[0]
    return jnp.maximum(out_field + bias_term[:, None, None], 0.0)


def reference(blk_temp, blk_qual, dest_tile, blk_offset, background, reflect, land, conv_first, bias_first, conv_second, bias_second, conv_third, bias_third, head):
    rows_all = background.shape[0]
    cols_all = background.shape[1]
    zero_index = jnp.zeros((), jnp.int32)

    def add_block(block_index, partial_value):
        numerator, denominator = partial_value
        first_row = (dest_tile[block_index] * TR + blk_offset[block_index]).astype(jnp.int32)
        quality = blk_qual[block_index].astype(jnp.float32)
        weighted = quality * blk_temp[block_index].astype(jnp.float32)
        numerator = lax.dynamic_update_slice(numerator, lax.dynamic_slice(numerator, (first_row, zero_index), (BR, cols_all)) + weighted, (first_row, zero_index))
        denominator = lax.dynamic_update_slice(denominator, lax.dynamic_slice(denominator, (first_row, zero_index), (BR, cols_all)) + quality, (first_row, zero_index))
        return numerator, denominator

    start_num = prior_weight * background
    start_den = jnp.full(background.shape, prior_weight, background.dtype)
    numerator, denominator = lax.fori_loop(0, NBLK, add_block, (start_num, start_den))
    blended = numerator / denominator
    margin = RADIUS + 3
    blended_pad = jnp.pad(blended, margin)
    reflect_pad = jnp.pad(reflect, ((0, 0), (margin, margin), (margin, margin)))
    land_pad = jnp.pad(land, margin)
    weights = gauss_taps()

    def band_fields(band_index):
        first_row = (band_index * TR).astype(jnp.int32)
        blended_band = lax.dynamic_slice_in_dim(blended_pad, first_row, TR + 2 * margin, 0)
        reflect_band = lax.dynamic_slice_in_dim(reflect_pad, first_row, TR + 2 * margin, 1).astype(jnp.float32)
        land_band = lax.dynamic_slice_in_dim(land_pad, first_row, TR + 2 * margin, 0).astype(blended.dtype)
        raw_full = jnp.concatenate([blended_band[None], reflect_band.astype(blended.dtype)], axis=0)
        smooth_ext = blur(raw_full, weights)
        raw_ext = raw_full[:, RADIUS:-RADIUS, RADIUS:-RADIUS]
        land_ext = land_band[RADIUS:-RADIUS, RADIUS:-RADIUS]
        return raw_ext, smooth_ext, land_ext

    def band_sums(band_index):
        raw_ext, smooth_ext, land_ext = band_fields(band_index)
        return fit(smooth_ext[:, 3:-3, 3:-3], land_ext[3:-3, 3:-3])

    normals, rights = lax.map(band_sums, jnp.arange(NT, dtype=jnp.int32))
    normal = jnp.sum(normals, axis=0)
    right_side = jnp.sum(rights, axis=0)
    fit_coefs = solve_small(normal + ridge_term * jnp.eye(NBANDS + 1, dtype=normal.dtype), right_side)
    kernels = ((conv_first, bias_first), (conv_second, bias_second), (conv_third, bias_third))

    def band_out(band_index):
        raw_ext, smooth_ext, land_ext = band_fields(band_index)
        base_ext, stack_ext = build_stack(raw_ext, smooth_ext, land_ext, fit_coefs)
        row_ids = band_index * TR + jnp.arange(TR + 6, dtype=jnp.int32) - 3
        col_ids = jnp.arange(cols_all + 6, dtype=jnp.int32) - 3
        inside = ((row_ids >= 0) & (row_ids < rows_all))[:, None] & ((col_ids >= 0) & (col_ids < cols_all))[None, :]
        hidden = jnp.where(inside[None], stack_ext, 0.0).astype(jnp.bfloat16)
        for layer_index in range(3):
            out_field = convolve(hidden, kernels[layer_index][0], kernels[layer_index][1])
            keep = inside[layer_index + 1:inside.shape[0] - layer_index - 1, layer_index + 1:inside.shape[1] - layer_index - 1]
            hidden = jnp.where(keep[None], out_field, 0.0).astype(jnp.bfloat16)
        correction = jnp.einsum("c,chw->hw", head.astype(jnp.float32), hidden.astype(jnp.float32), precision=highest)
        return base_ext[3:-3, 3:-3] + land_ext[3:-3, 3:-3] * correction

    sharp_temp = lax.map(band_out, jnp.arange(NT, dtype=jnp.int32)).reshape(rows_all, cols_all)
    return sharp_temp, fit_coefs
```

```python
import jax
import jax.numpy as jnp
import numpy as np
from jax import lax
from jax.experimental import pallas as pl
from jax.experimental.pallas import tpu as pltpu
from jax.sharding import PartitionSpec as P

TR = 512
BR = 128
RADIUS = 7
NBANDS = 6
CH = 16
NX = 4
NZ = 4
NY = 4
LANES = 128
HALO = 16
WIN = TR + 2 * HALO
ACC = WIN + 2 * HALO
QROWS = TR // NY
RQ = QROWS + 2 * HALO
COLS = NY * LANES
GROUPS = RQ // 8
KROWS = CH * 8 + 2 * CH
STRIP = 64
STEPS = 6
STRIPS = TR // STRIP

prior_weight = 0.5
ridge_term = 1.0
f32 = jnp.float32
bf16 = jnp.bfloat16
VMEM = pl.BlockSpec(memory_space=pltpu.VMEM)
SMEM = pl.BlockSpec(memory_space=pltpu.SMEM)
ANY = pl.BlockSpec(memory_space=pl.ANY)


def tile_id(x, z, c):
    return (x * NZ + z) * 2 + c


def along_y(k):
    return [(i, (i + k) % NY) for i in range(NY)]


def along_x(k):
    return [
        (tile_id(x, z, c), tile_id((x + k) % NX, z, c))
        for x in range(NX)
        for z in range(NZ)
        for c in range(2)
    ]


def along_z(k):
    return [
        (tile_id(x, z, c), tile_id(x, (z + k) % NZ, c))
        for x in range(NX)
        for z in range(NZ)
        for c in range(2)
    ]


core_pair = [(i, i ^ 1) for i in range(2 * NX * NZ)]


def call(kernel, outs, ins, scratch=(), flops=0, nbytes=0, name=None, grid=(), place=VMEM, alias={}):
    return pl.pallas_call(
        kernel,
        grid=grid,
        out_shape=outs,
        in_specs=ins,
        out_specs=place
        if isinstance(place, tuple)
        else jax.tree.map(lambda o: SMEM if o.shape == (NBANDS + 1,) else place, outs),
        scratch_shapes=list(scratch),
        input_output_aliases=alias,
        compiler_params=pltpu.CompilerParams(vmem_limit_bytes=56 * 1024 * 1024),
        cost_estimate=pl.CostEstimate(flops=flops, bytes_accessed=nbytes, transcendentals=0),
        name=name,
    )


def sds(shape, dtype):
    return jax.ShapeDtypeStruct(shape, dtype)


def add_blocks(meta, info, count, arrivals, add):
    c = info[2]
    for piece in range(8):
        arrivals[piece].wait()

        def body(j, carry, piece=piece):
            code = meta[piece, j]
            tile = code >> 9
            off = code & (TR - 1)
            mine = (tile & 1) == c

            @pl.when(mine)
            def _():
                add(piece, j, tile >> 1, off + 2 * HALO, 0, BR)

            @pl.when(jnp.logical_not(mine) & ((off > TR - BR - HALO) | (off < HALO)))
            def _():
                @pl.when((off > TR - BR - HALO) & (tile < 2 * NX * NZ - 1))
                def _():
                    add(piece, j, (tile + 1) >> 1, off - (TR - BR - HALO), BR - HALO, HALO)

                @pl.when((off < HALO) & (tile > 0))
                def _():
                    add(piece, j, (tile - 1) >> 1, off + 2 * HALO + TR, 0, HALO)

            return carry

        lax.fori_loop(0, count, body, 0, unroll=2)


def pack_kernel(info, dest, offset, temp, qual, *outs):
    s = info[3]
    count = temp.shape[0]
    lane = lax.broadcasted_iota(jnp.int32, (HALO, LANES), 1)
    row = lax.broadcasted_iota(jnp.int32, (HALO, LANES), 0)
    places = jnp.zeros((HALO, LANES), jnp.int32)
    for j in range(count):
        numbers = (dest[j], offset[j] >> 4, offset[j] & 15)
        for i, number in enumerate(numbers):
            places = jnp.where((lane == j) & (row == i), number, places)
    places = places.astype(f32).astype(bf16)
    for k, out in enumerate(outs):
        lanes = pl.ds(pl.multiple_of(lax.rem(s + k, NY) * LANES, LANES), LANES)
        for j in range(count):
            out[BR * j : BR * (j + 1), :] = qual[j, :, lanes]
            out[BR * (count + j) : BR * (count + j + 1), :] = temp[j, :, lanes]
        out[2 * count * BR :, :] = places

def scatter_kernel(info, *refs):
    pieces, outs = refs[0:8], refs[9:17]
    acc_n, acc_d, places, meta, sem, held, numbers, staged, in_sems, place_sems, out_sems = refs[17:]
    x, z = info[0], info[1]
    count = (pieces[0].shape[0] - HALO) // (2 * BR)
    small, large = [], []
    for i, piece in enumerate(pieces):
        tail = piece.at[pl.ds(2 * count * BR, HALO)]
        small.append(pltpu.make_async_copy(tail, numbers.at[i], place_sems.at[i]))
        small[i].start()
    for i, piece in enumerate(pieces):
        body = piece.at[pl.ds(0, 2 * count * BR)]
        large.append(pltpu.make_async_copy(body, held.at[i], in_sems.at[i]))
        large[i].start()
    for i in range(8):
        small[i].wait()
        number = numbers[i].astype(f32)
        code = number[0:1] * TR + number[1:2] * 16.0 + number[2:3]
        places[i : i + 1, :] = code.astype(jnp.int32)
    copy = pltpu.make_async_copy(places, meta, sem)
    copy.start()

    def clear(i, carry):
        acc_n[i] = jnp.zeros((ACC, LANES), f32)
        acc_d[i] = jnp.zeros((ACC, LANES), f32)
        return carry

    def add(piece, j, slot, start, row, rows):
        span = pl.ds(start, rows)
        at = pl.multiple_of(j * BR + row, HALO)
        q = held[piece, pl.ds(at, rows), :].astype(f32)
        t = held[piece, pl.ds(count * BR + at, rows), :].astype(f32)
        acc_d[slot, span, :] = acc_d[slot, span, :] + q
        acc_n[slot, span, :] = acc_n[slot, span, :] + q * t

    lax.fori_loop(0, NX * NZ, clear, 0)
    copy.wait()
    add_blocks(meta, info, count, large, add)
    leaving = []
    for kx in range(NX):
        for kz in range(NZ):
            slot = lax.rem(x + kx, NX) * NZ + lax.rem(z + kz, NZ)
            targets = (outs[kx].at[kz], outs[NX + kz].at[kx])
            for acc, target in zip((acc_n, acc_d), targets):
                i = len(leaving)
                staged[i] = acc[slot, HALO : HALO + WIN, :].astype(bf16)
                leaving.append(pltpu.make_async_copy(staged.at[i], target, out_sems.at[i]))
                leaving[i].start()
    for copy in leaving:
        copy.wait()


def scatter_scratch(rows):
    return [pltpu.VMEM((NX * NZ, ACC, LANES), f32)] * 2 + [
        pltpu.VMEM((8, LANES), jnp.int32),
        pltpu.SMEM((8, LANES), jnp.int32),
        pltpu.SemaphoreType.DMA,
        pltpu.VMEM((8, rows, LANES), bf16),
        pltpu.VMEM((8, HALO, LANES), bf16),
        pltpu.VMEM((2 * NX * NZ, WIN, LANES), bf16),
        pltpu.SemaphoreType.DMA((8,)),
        pltpu.SemaphoreType.DMA((8,)),
        pltpu.SemaphoreType.DMA((2 * NX * NZ,)),
    ]


def sum_kernel(a, b, c, d, *refs):
    for k, out in enumerate(refs[-4:]):
        out[...] = (a[k].astype(f32) + b[k].astype(f32)) + (c[k].astype(f32) + d[k].astype(f32))


def order_kernel(*refs):
    pass


def slab_kernel(reflect, land, first, last):
    lane = lax.broadcasted_iota(jnp.int32, (STRIP, LANES), 1)

    for plane in range(NBANDS + 1):
        sides = [jnp.zeros((STRIP, LANES), f32) for _ in range(2)]
        for i in range(STRIPS):
            rows = slice(STRIP * i, STRIP * (i + 1))
            cells = (reflect[plane, rows, :] if plane < NBANDS else land[rows, :]).astype(f32)
            for side, source in enumerate((0, LANES - HALO)):
                moved = pltpu.roll(cells, (HALO * i - source) % LANES, 1)
                sides[side] = jnp.where(lane >> 4 == i, moved, sides[side])
        first[plane] = sides[0].astype(bf16)
        last[plane] = sides[1].astype(bf16)


def beside_of(left, right, i):
    lane = lax.broadcasted_iota(jnp.int32, left.shape, 1)
    after = pltpu.roll(right, (-HALO * i) % LANES, 1)
    before = pltpu.roll(left, (HALO - HALO * i) % LANES, 1)
    return jnp.where(lane < HALO, after, jnp.where(lane < 2 * HALO, before, 0.0)).astype(bf16)


def edges_kernel(r0, r1, l0, l1, b0, b1, left, right, top, bottom):
    own = slice(0, LANES)
    sides = ((top, r0, l0, b0, 0, 0), (bottom, r1, l1, b1, STRIPS - 1, STRIP - HALO))
    for out, reflect, land, background, strip, row in sides:
        out[0:NBANDS, :, own] = reflect[...]
        out[NBANDS, :, own] = land[...].astype(f32).astype(bf16)
        high, low = split(background[...])
        out[NBANDS + 1, :, own] = high
        out[NBANDS + 2, :, own] = low
        for plane in range(NBANDS + 1):
            rows = slice(row, row + HALO)
            out[plane, :, LANES:] = beside_of(
                left[plane, rows, :].astype(f32), right[plane, rows, :].astype(f32), strip
            )
        for plane in range(NBANDS + 1, NBANDS + 3):
            out[plane, :, LANES:] = jnp.zeros((HALO, LANES), bf16)


def adjoint_kernel(
    reflect, land, above, below, left, right, row_h, row_l, col_h, col_l,
    adjoint, normal, window, beside, bands,
):
    for rows, edge in ((slice(0, HALO), above), (slice(HALO + TR, WIN), below)):
        window[:, rows, :] = edge[0 : NBANDS + 1, :, 0:LANES]
        beside[:, rows, :] = edge[0 : NBANDS + 1, :, LANES:]
    window[0:NBANDS, HALO : HALO + TR, :] = reflect[...]
    window[NBANDS, HALO : HALO + TR, :] = land[...].astype(f32).astype(bf16)

    def spread(plane, carry):
        before = left[plane].astype(f32)
        after = right[plane].astype(f32)
        for i in range(STRIPS):
            rows = slice(HALO + STRIP * i, HALO + STRIP * (i + 1))
            beside[plane, rows, :] = beside_of(before, after, i)
        return carry

    lax.fori_loop(0, NBANDS + 1, spread, 0)
    pairs = [(i, j) for i in range(NBANDS + 1) for j in range(i, NBANDS + 1)]
    own = slice(HALO, HALO + QROWS)

    def quarter(q, sums):
        rows = pl.ds(pl.multiple_of(QROWS * q, QROWS), RQ)

        def cells(plane):
            return jnp.concatenate([window[plane, rows, :], beside[plane, rows, :]], axis=1)

        land = cells(NBANDS).astype(f32)
        for band in range(NBANDS):
            x = cells(band)
            down = split(dot(row_h[...], x) + dot(row_l[...], x))
            bands[band] = dot3(down, (col_h[...], col_l[...]))
        for i in range(NBANDS + 1):
            value = split(land if i == 0 else land * bands[i - 1])
            down = split(dot3((row_h[own, :], row_l[own, :]), value))
            adjoint[i, pl.ds(pl.multiple_of(QROWS * q, QROWS), QROWS), :] = dot3(
                down, (col_h[:, 0:LANES], col_l[:, 0:LANES])
            )

        def step(g, sums):
            at = pl.multiple_of(HALO + 16 * g, 16)
            part = pl.ds(at, 16)
            mask = window[NBANDS, pl.ds(pl.multiple_of(QROWS * q + at, 16), 16), :].astype(f32)
            x = [None] + [bands[band, part, 0:LANES] for band in range(NBANDS)]
            mx = [mask] + [mask * x[i] for i in range(1, NBANDS + 1)]
            new = []
            for (i, j), total in zip(pairs, sums):
                v = mx[j] if i == 0 else mx[i] * x[j]
                new.append(total + (v[0:8] + v[8:16]))
            return tuple(new)

        return lax.fori_loop(0, QROWS // 16, step, sums)

    sums = lax.fori_loop(0, NY, quarter, tuple(jnp.zeros((8, LANES), f32) for _ in pairs))
    row = lax.broadcasted_iota(jnp.int32, (8, LANES), 0)
    lane = lax.broadcasted_iota(jnp.int32, (8, LANES), 1)
    result = jnp.zeros((8, LANES), f32)
    for (i, j), total in zip(pairs, sums):
        here = ((row == i) & (lane == j)) | ((row == j) & (lane == i))
        result = jnp.where(here, jnp.sum(total), result)
    normal[...] = result


def cut_kernel(window, after, out):
    for k in range(NY):
        out[k] = window[:, QROWS * k : QROWS * k + RQ, :]


def blend_kernel(info, *refs):
    nums, dens = refs[0:4], refs[4:8]
    background, above, below = refs[8:11]
    adjoint, normal = refs[11], refs[12]
    outs, field = refs[13:17], refs[17]
    first, last, s = info[4], info[5], info[3]
    num = nums[0][...].astype(f32)
    den = dens[0][...].astype(f32)
    for n in nums[1:]:
        num = num + n[...].astype(f32)
    for d in dens[1:]:
        den = den + d[...].astype(f32)
    ends = [
        edge[NBANDS + 1, :, 0:LANES].astype(f32) + edge[NBANDS + 2, :, 0:LANES].astype(f32) for edge in (above, below)
    ]
    prior = jnp.concatenate([ends[0], background[...], ends[1]], axis=0)
    row = lax.broadcasted_iota(jnp.int32, (WIN, LANES), 0)
    inside = (row >= HALO * first) & (row < WIN - HALO * last)
    blended = (prior_weight * prior + num) / (prior_weight + den)
    field[...] = jnp.where(inside, blended, 0.0)
    totals = [jnp.zeros((8, LANES), f32) for _ in range(NBANDS + 1)]

    def step(g, totals):
        cells = field[pl.ds(pl.multiple_of(HALO + 16 * g, 16), 16), :]
        rows = pl.ds(pl.multiple_of(16 * g, 16), 16)
        new = []
        for i, total in enumerate(totals):
            v = cells * adjoint[i, rows, :]
            new.append(total + (v[0:8] + v[8:16]))
        return tuple(new)

    totals = lax.fori_loop(0, TR // 16, step, tuple(totals))
    row = lax.broadcasted_iota(jnp.int32, (8, LANES), 0)
    lane = lax.broadcasted_iota(jnp.int32, (8, LANES), 1)
    sums = normal[...]
    for i, total in enumerate(totals):
        sums = jnp.where((row == i) & (lane == NBANDS + 1), jnp.sum(total), sums)
    for k, out in enumerate(outs):
        start = pl.multiple_of(lax.rem(s + k, NY) * QROWS, QROWS)
        out[0:RQ, :] = field[pl.ds(start, RQ), :]
        out[RQ:, :] = sums


def merge_kernel(b0, b1, b2, b3, out):
    total = (b0[...] + b2[...]) + (b1[...] + b3[...])
    out[...] = jnp.broadcast_to(total[None], out.shape)


def lane_place(s, k):
    return pl.ds(pl.multiple_of(lax.rem(s + NY - k, NY) * LANES, LANES), LANES)


def split(v):
    high = v.astype(bf16)
    return high, (v - high.astype(f32)).astype(bf16)


def dot(a, b):
    return jnp.dot(a, b, preferred_element_type=f32)


def dot3(a, b):
    return dot(a[0], b[0]) + (dot(a[0], b[1]) + dot(a[1], b[0]))


def row_inside(info, rows):
    row = lax.broadcasted_iota(jnp.int32, (rows, 1), 0)
    return (row >= HALO * info[6]) & (row < rows - HALO * info[7])


def bands_kernel(info, pieces, row_h, row_l, col_h, col_l, turn, fields, coarse, raw):
    for k in range(NY):
        raw[:, :, LANES * k : LANES * (k + 1)] = pieces[k]
    inside = row_inside(info, RQ)
    for band in range(NBANDS + 1):
        cells = raw[band]
        fields[band] = dot(cells, turn[...]).astype(bf16)
        if band < NBANDS:
            down = split(dot(row_h[...], cells) + dot(row_l[...], cells))
            coarse[band] = jnp.where(inside, dot3(down, (col_h[...], col_l[...])), 0.0)


def write(slot, start, value):
    rows = slice(start, start + value.shape[0])
    lane = lax.broadcasted_iota(jnp.int32, (value.shape[0], LANES), 1)
    for t in range(NY):
        slot[t + 1, rows, :] = value[:, LANES * t : LANES * (t + 1)]
    before = pltpu.roll(value[:, 3 * LANES :], 1, 1)
    after = pltpu.roll(value[:, :LANES], LANES - 1, 1)
    slot[0, rows, :] = jnp.where(lane > 0, before, 0.0)
    slot[5, rows, :] = jnp.where(lane < LANES - 1, after, 0.0)


def put(slot, g, hidden):
    for t in range(6):
        part = slice(LANES * t, LANES * (t + 1))
        hidden[g, 0:128, part] = slot[t].astype(bf16)
        hidden[g + 1, 128:144, part] = slot[t, pl.ds(7, CH, stride=8), :].astype(bf16)
        hidden[g - 1, 144:160, part] = slot[t, pl.ds(0, CH, stride=8), :].astype(bf16)


def clear_ends(hidden):
    zero_rows = jnp.zeros((CH, 6 * LANES), bf16)
    hidden[1, 128:144, :] = zero_rows
    hidden[GROUPS - 2, 144:160, :] = zero_rows


def assemble_kernel(
    info, b0, b1, b2, b3, row_h, row_l, col_h, col_l, turn, fields_in, bands_in,
    coarse, hidden_out, natural, blended, group, fields, bands, hidden, in_sems, out_sems,
):
    s = info[3]
    arrays = ((fields_in, fields), (bands_in, bands))
    copies = [pltpu.make_async_copy(a, b, in_sems.at[i]) for i, (a, b) in enumerate(arrays)]
    for copy in copies:
        copy.start()
    for k, piece in enumerate((b0, b1, b2, b3)):
        natural[:, lane_place(s, k)] = piece[0:RQ, :]
    high, low = split(natural[...])
    down = split(dot3((row_h[...], row_l[...]), (high, low)))
    coarse[...] = jnp.where(
        row_inside(info, RQ), dot3(down, (col_h[...], col_l[...])), 0.0
    )
    blended[...] = dot(high, turn[...])
    clear_ends(hidden)
    for copy in copies:
        copy.wait()

    def leave(m):
        part = pl.ds(2 * m - 1, 2)
        return pltpu.make_async_copy(hidden.at[part], hidden_out.at[part], out_sems.at[m])

    def step(m, carry):
        rows = pl.ds(pl.multiple_of(16 * m, 16), 16)
        values = [jnp.zeros((16, COLS), f32), blended[rows, :], coarse[rows, :]]
        values.append(fields[NBANDS, rows, :].astype(f32))
        values += [fields[band, rows, :].astype(f32) for band in range(NBANDS)]
        values += [bands[band, rows, :] for band in range(NBANDS)]
        for half in range(2):
            g = 2 * m + half
            for channel, value in enumerate(values):
                write(group.at[half], 8 * channel, value[8 * half : 8 * half + 8])

            @pl.when((g >= 1) & (g <= GROUPS - 2))
            def _():
                put(group.at[half], g, hidden)

        @pl.when(m >= 1)
        def _():
            leave(m).start()

        return carry

    lax.fori_loop(0, GROUPS // 2, step, 0)
    for m in range(1, GROUPS // 2):
        leave(m).wait()


def assemble_scratch():
    return [
        pltpu.VMEM((RQ, COLS), f32),
        pltpu.VMEM((RQ, COLS), f32),
        pltpu.VMEM((2, 6, CH * 8, LANES), f32),
        pltpu.VMEM((NBANDS + 1, RQ, COLS), bf16),
        pltpu.VMEM((NBANDS, RQ, COLS), f32),
        pltpu.VMEM((GROUPS, KROWS, 6 * LANES), bf16),
        pltpu.SemaphoreType.DMA((2,)),
        pltpu.SemaphoreType.DMA((GROUPS // 2,)),
    ]


def solve(sums):
    row = lax.broadcasted_iota(jnp.int32, (8, LANES), 0)
    lane = lax.broadcasted_iota(jnp.int32, (8, LANES), 1)
    work = sums + jnp.where((row == lane) & (row <= NBANDS), ridge_term, 0.0)
    for pivot in range(NBANDS + 1):
        pivot_row = work[pivot : pivot + 1, :]
        pivot_value = jnp.sum(jnp.where(lane[0:1] == pivot, pivot_row, 0.0), axis=1, keepdims=True)
        scaled = pivot_row / pivot_value
        factor = jnp.sum(jnp.where(lane == pivot, work, 0.0), axis=1, keepdims=True)
        work = jnp.where(row == pivot, scaled, work - factor * scaled)
    picked = jnp.where(lane == NBANDS + 1, work, 0.0)
    return [jnp.sum(picked[i : i + 1, :]) for i in range(NBANDS + 1)]


def main_kernel(
    info, head, sums, coarse_in, fields_in, bands_in, kernels, biases, turn_back_in, stacked_in,
    o0, o1, o2, o3, fit_out, first_h, second_h, group, base, result,
    coarse, fields, bands, turn_back, stacked, sems, stack_sems,
):
    s = info[3]
    arrays = ((coarse_in, coarse), (fields_in, fields), (bands_in, bands))
    copies = [pltpu.make_async_copy(a, b, sems.at[i]) for i, (a, b) in enumerate(arrays)]
    for copy in copies:
        copy.start()
    steps = STEPS

    def stack_copy(i):
        part = pl.ds(1 + steps * i, steps)
        return pltpu.make_async_copy(stacked_in.at[part], stacked.at[part], stack_sems.at[i])

    for i in range((GROUPS - 2) // steps):
        stack_copy(i).start()
    turn_copy = pltpu.make_async_copy(turn_back_in, turn_back, sems.at[3])
    turn_copy.start()
    coefs = solve(jnp.sum(sums[...], axis=0))
    for i in range(NBANDS + 1):
        fit_out[i] = coefs[i]
    for copy in copies:
        copy.wait()
    clear_ends(first_h)
    clear_ends(second_h)

    def start(m, carry):
        rows = pl.ds(pl.multiple_of(16 * m, 16), 16)
        value = coarse[rows, :]
        for band in range(NBANDS):
            value = value + coefs[band + 1] * (
                fields[band, rows, :].astype(f32) - bands[band, rows, :]
            )
        lane = lax.broadcasted_iota(jnp.int32, (16, LANES), 1)
        base[rows, LANES : 5 * LANES] = value
        base[rows, 0:LANES] = jnp.where(lane > 0, pltpu.roll(value[:, 3 * LANES :], 1, 1), 0.0)
        base[rows, 5 * LANES :] = jnp.where(
            lane < LANES - 1, pltpu.roll(value[:, :LANES], LANES - 1, 1), 0.0
        )
        return carry

    lax.fori_loop(0, GROUPS // 2, start, 0)
    edge_row = lax.broadcasted_iota(jnp.int32, (CH, 6 * LANES), 0) == 0

    def with_base(g):
        own = stacked[g, 0:16, :].astype(f32)
        at = pl.multiple_of(8 * g, 8)
        own = jnp.concatenate([base[pl.ds(at, 8), :], own[8:16]], axis=0).astype(bf16)
        above = jnp.where(
            edge_row, base[pl.ds(8 * g - 1, 1), :], stacked[g, 128:144, :].astype(f32)
        )
        below = jnp.where(
            edge_row, base[pl.ds(8 * g + 8, 1), :], stacked[g, 144:160, :].astype(f32)
        )
        return jnp.concatenate(
            [own, stacked[g, 16:128, :], above.astype(bf16), below.astype(bf16)], axis=0
        )

    def convolved(layer, cells):
        spans = [slice(LANES * b, LANES * (b + 4)) for b in range(3)]
        taps = jnp.concatenate(
            [cells[0:128, span] for span in spans] + [cells[128:160, span] for span in spans],
            axis=0,
        )
        bias = jnp.concatenate([biases[layer]] * NY, axis=1)
        return jnp.maximum(dot(kernels[layer], taps) + bias, 0.0)

    for layer, following in enumerate((first_h, second_h)):

        def body(i, carry, layer=layer, following=following):
            if layer == 0:
                stack_copy(i).wait()
            for u in range(steps):
                g = 1 + steps * i + u
                cells = with_base(g) if layer == 0 else first_h[g]
                outside = ((g == 1) & (info[6] == 1)) | ((g == GROUPS - 2) & (info[7] == 1))
                keep = jnp.where(outside, 0.0, 1.0)
                write(group.at[u], 0, convolved(layer, cells) * keep)
                put(group.at[u], g, following)
            return carry

        lax.fori_loop(0, (GROUPS - 2) // steps, body, 0)

    def last(i, carry):
        mask = fields[NBANDS, pl.ds(pl.multiple_of(HALO + 32 * i, 32), 32), :].astype(f32)
        for u in range(4):
            g = 2 + 4 * i + u
            third = convolved(2, second_h[g]).astype(bf16).astype(f32)
            total = head[0] * third[0:8]
            for channel in range(1, CH):
                total = total + head[channel] * third[8 * channel : 8 * channel + 8]
            rows = pl.ds(pl.multiple_of(8 * g, 8), 8)
            out_rows = pl.ds(pl.multiple_of(8 * g - HALO, 8), 8)
            result[out_rows, :] = (
                base[rows, LANES : 5 * LANES] + mask[8 * u : 8 * u + 8] * total
            )
        return carry

    lax.fori_loop(0, QROWS // 32, last, 0)
    turn_copy.wait()
    high, low = split(result[...])
    result[...] = dot(high, turn_back[...]) + dot(low, turn_back[...])
    for k, out in enumerate((o0, o1, o2, o3)):
        out[...] = result[:, pl.ds(pl.multiple_of(lax.rem(s + k, NY) * LANES, LANES), LANES)]


def main_scratch():
    hidden = pltpu.VMEM((GROUPS, KROWS, 6 * LANES), bf16)
    return [
        hidden,
        hidden,
        pltpu.VMEM((STEPS, 6, CH * 8, LANES), f32),
        pltpu.VMEM((RQ, 6 * LANES), f32),
        pltpu.VMEM((QROWS, COLS), f32),
        pltpu.VMEM((RQ, COLS), f32),
        pltpu.VMEM((NBANDS + 1, RQ, COLS), bf16),
        pltpu.VMEM((NBANDS, RQ, COLS), f32),
        pltpu.VMEM((COLS, COLS), bf16),
        hidden,
        pltpu.SemaphoreType.DMA((4,)),
        pltpu.SemaphoreType.DMA(((GROUPS - 2) // STEPS,)),
    ]


def join_kernel(info, o0, o1, o2, o3, out):
    s = info[3]
    for k, piece in enumerate((o0, o1, o2, o3)):
        start = pl.multiple_of(lax.rem(s + NY - k, NY) * QROWS, QROWS)
        out[pl.ds(start, QROWS), :] = piece[...]


def band_matrix(rows, columns):
    offsets = np.arange(2 * RADIUS + 1) - RADIUS
    norm = np.sum(np.exp(-0.125 * offsets**2))
    apart = rows[:, None] - columns[None, :]
    weights = np.where(np.abs(apart) <= RADIUS, np.exp(-0.125 * apart**2) / norm, 0.0)
    high = weights.astype(bf16)
    return jnp.asarray(high), jnp.asarray((weights - high.astype(np.float64)).astype(bf16))


def matrices_kernel(taps, bias, kernels, biases):
    def iota(size, axis):
        return lax.broadcasted_iota(jnp.int32, (size, size), axis)

    tall = (CH * 8, CH)
    spread_rows = (
        lax.broadcasted_iota(jnp.int32, tall, 0) >> 3 == lax.broadcasted_iota(jnp.int32, tall, 1)
    )
    spread_rows = jnp.where(spread_rows, 1.0, 0.0).astype(bf16)
    wide = (CH, CH * 8)
    channel, lane = (lax.broadcasted_iota(jnp.int32, wide, a) for a in range(2))
    spread_lanes = jnp.where(lane >> 3 == channel, 1.0, 0.0).astype(bf16)
    r, l = iota(CH * 8, 0), iota(CH * 8, 1)
    up = (l & 7) - (r & 7)
    for layer in range(3):
        halo = jnp.zeros((CH * 8, CH * 8), f32)
        for b in range(3):
            own = jnp.zeros((CH * 8, CH * 8), f32)
            for a in range(3):
                column = dot(spread_rows, taps[layer, a, b]).astype(bf16)
                own = jnp.where(up == a - 1, dot(column, spread_lanes), own)
                if a == 1:
                    continue
                at = 32 * b + (0 if a == 0 else CH)
                placed = jnp.where(lane == channel + at, 1.0, 0.0).astype(bf16)
                halo = halo + jnp.where((r & 7) == (0 if a == 0 else 7), dot(column, placed), 0.0)
            kernels[layer, :, 128 * b : 128 * b + 128] = own.astype(bf16)
        kernels[layer, :, 384:480] = halo[:, 0:96].astype(bf16)
        for o in range(CH):
            biases[layer, 8 * o : 8 * o + 8, :] = jnp.broadcast_to(
                bias[CH * layer + o : CH * layer + o + 1, :], (8, LANES)
            )


def exchange(pieces, axis, route):
    return [pieces[0]] + [lax.ppermute(pieces[k], axis, route(k)) for k in range(1, 4)]


def shards(
    blk_temp, blk_qual, dest_tile, blk_offset, background, reflect, land,
    conv_first, bias_first, conv_second, bias_second, conv_third, bias_third, head,
):
    tile = lax.axis_index("tiles")
    s = lax.axis_index("swath")
    tiles = lax.axis_size("tiles")
    x, z, c = tile // (2 * NZ), (tile // 2) % NZ, tile % 2
    first = tile == 0
    last = tile == tiles - 1
    info = jnp.stack(
        [x, z, c, s, first, last, first & (s == 0), last & (s == NY - 1)]
    ).astype(jnp.int32)

    count = blk_temp.shape[0]
    down = [(i, i + 1) for i in range(tiles - 1)]
    up = [(i + 1, i) for i in range(tiles - 1)]

    def edge(last_rows):
        at = TR // HALO - 1 if last_rows else 0
        return [
            pl.BlockSpec((NBANDS, HALO, LANES), lambda i: (0, at, 0)),
            pl.BlockSpec((HALO, LANES), lambda i: (at, 0)),
            pl.BlockSpec((HALO, LANES), lambda i: (at, 0)),
        ]

    edges = [spec for pair in zip(edge(False), edge(True)) for spec in pair]
    row_h, row_l = band_matrix(np.arange(RQ), np.arange(RQ))
    natural = np.arange(COLS)
    place = NY * (natural % LANES) + natural // LANES
    col_h, col_l = band_matrix(natural, place)
    turn = jnp.asarray((natural[:, None] == place[None, :]).astype(bf16))
    turn_back = jnp.asarray((place[:, None] == natural[None, :]).astype(bf16))
    lanes = np.arange(2 * LANES)
    spot = np.where(lanes < LANES + HALO, lanes, lanes - LANES - 2 * HALO)
    spot = np.where(lanes < LANES + 2 * HALO, spot, 1000 * lanes)
    near_h, near_l = band_matrix(spot, spot)

    strip = sds((NBANDS + 1, STRIP, LANES), bf16)
    first_columns, last_columns = call(slab_kernel, (strip, strip), [VMEM] * 2, name="slab")(
        reflect, land
    )
    from_left = lax.ppermute(last_columns, "swath", [(i, i + 1) for i in range(NY - 1)])
    from_right = lax.ppermute(first_columns, "swath", [(i + 1, i) for i in range(NY - 1)])
    packed = call(
        pack_kernel,
        (sds((2 * count * BR + HALO, LANES), bf16),) * 4,
        [SMEM] * 3 + [VMEM] * 2,
        name="pack",
    )(info, dest_tile, blk_offset, blk_temp, blk_qual)
    block = sds(packed[0].shape, bf16)
    packed = tuple(packed[0:1]) + tuple(call(
        order_kernel, (block,) * 3, [ANY] * 5, place=ANY, alias={0: 0, 1: 1, 2: 2}, name="order"
    )(*packed[1:], from_left, from_right))
    edge_rows = sds((NBANDS + 3, HALO, 2 * LANES), bf16)
    top, bottom = call(
        edges_kernel, (edge_rows,) * 2, edges + [VMEM] * 2, grid=(1,), name="edges"
    )(reflect, reflect, land, land, background, background, from_left, from_right)
    above = lax.ppermute(bottom, "tiles", down)
    below = lax.ppermute(top, "tiles", up)

    adjoint, normal, window = call(
        adjoint_kernel,
        (
            sds((NBANDS + 1, TR, LANES), f32),
            sds((8, LANES), f32),
            sds((NBANDS + 1, WIN, LANES), bf16),
        ),
        [VMEM] * 10,
        scratch=[
            pltpu.VMEM((NBANDS + 1, WIN, LANES), bf16),
            pltpu.VMEM((NBANDS, RQ, 2 * LANES), f32),
        ],
        name="adjoint",
    )(reflect, land, above, below, from_left, from_right, row_h, row_l, near_h, near_l)
    taps = jnp.transpose(jnp.stack([conv_first, conv_second, conv_third]), (0, 3, 4, 1, 2))
    bias = jnp.concatenate([bias_first, bias_second, bias_third])
    kernels, biases = call(
        matrices_kernel,
        (sds((3, CH * 8, 3 * KROWS), bf16), sds((3, CH * 8, LANES), f32)),
        [VMEM] * 2,
        name="matrices",
    )(taps, jnp.broadcast_to(bias[:, None], (3 * CH, LANES)))
    weights = head.astype(f32)

    chip = exchange(packed, "swath", along_y)
    chip[1] = call(
        order_kernel, (block,), [ANY] * 3, place=ANY, alias={0: 0}, name="order"
    )(chip[1], adjoint, kernels)[0]
    chip = chip + [lax.ppermute(p, "tiles", core_pair) for p in chip]

    cut = call(
        cut_kernel,
        sds((NY, NBANDS + 1, RQ, LANES), bf16),
        [VMEM] + [ANY],
        name="cut",
    )(window, chip[2])
    pieces = lax.all_to_all(cut, "swath", split_axis=0, concat_axis=0, tiled=True)
    fields, bands = call(
        bands_kernel,
        (sds((NBANDS + 1, RQ, COLS), bf16), sds((NBANDS, RQ, COLS), f32)),
        [SMEM] + [VMEM] * 6,
        scratch=[pltpu.VMEM((NBANDS + 1, RQ, COLS), bf16)],
        flops=2 * 6 * 160 * 512 * (320 + 1536),
        nbytes=10 << 20,
        name="bands",
    )(info, pieces, row_h, row_l, col_h, col_l, turn)
    part = sds((4, WIN, LANES), bf16)
    routed = call(
        scatter_kernel,
        (part,) * 8,
        [SMEM] + [ANY] * 9,
        scratch=scatter_scratch(2 * count * BR),
        place=ANY,
        flops=96 * 128 * 128 * 8,
        nbytes=12 << 20,
        name="scatter",
    )(info, *chip, cut)
    nums = exchange(routed[0:4], "tiles", along_x)
    dens = exchange(routed[4:8], "tiles", along_z)

    one = sds((WIN, LANES), f32)
    summed = call(sum_kernel, (one,) * 4, [VMEM] * 4 + [ANY], nbytes=3 << 20, name="add")
    nums = summed(*nums, fields)
    dens = summed(*dens, fields)
    nums = exchange(nums, "tiles", along_z)
    dens = exchange(dens, "tiles", along_x)
    rows = call(
        blend_kernel,
        (sds((RQ + 8, LANES), f32),) * 4,
        [SMEM] + [VMEM] * 13,
        scratch=[pltpu.VMEM((WIN, LANES), f32)],
        nbytes=3 << 20,
        name="blend",
    )(info, *nums, *dens, background, above, below, adjoint, normal)
    rows = exchange(rows, "swath", along_y)
    sums = call(
        merge_kernel,
        sds((tiles, 8, LANES), f32),
        [pl.BlockSpec((8, LANES), lambda i: (RQ // 8, 0))] * 4,
        grid=(1,),
        name="merge",
    )(*rows)
    sums = lax.all_to_all(sums, "tiles", split_axis=0, concat_axis=0, tiled=True)
    coarse, stacked = call(
        assemble_kernel,
        (sds((RQ, COLS), f32), sds((GROUPS, KROWS, 6 * LANES), bf16)),
        [SMEM] + [VMEM] * 9 + [ANY] * 2,
        scratch=assemble_scratch(),
        place=(VMEM, ANY),
        flops=2 * 160 * 512 * (480 + 1536),
        nbytes=8 << 20,
        name="assemble",
    )(info, *rows, row_h, row_l, col_h, col_l, turn, fields, bands)
    *sharp, fit_coefs = call(
        main_kernel,
        (sds((QROWS, LANES), f32),) * 4 + (sds((NBANDS + 1,), f32),),
        [SMEM, SMEM, VMEM] + [ANY] * 3 + [VMEM] * 2 + [ANY] * 2,
        scratch=main_scratch(),
        flops=3 * 18 * 2 * 384 * 160 * 512,
        nbytes=8 << 20,
        name="convolve",
    )(info, weights, sums, coarse, fields, bands, kernels, biases, turn_back, stacked)
    sharp = exchange(sharp, "swath", along_y)
    out = call(join_kernel, sds((TR, LANES), f32), [SMEM] + [VMEM] * 4, name="join")(info, *sharp)
    return out, fit_coefs


def solution(mesh):
    placed = (
        P(("tiles", "swath"), None, None),
        P(("tiles", "swath"), None, None),
        P(("tiles", "swath")),
        P(("tiles", "swath")),
        P("tiles", "swath"),
        P(None, "tiles", "swath"),
        P("tiles", "swath"),
        P(),
        P(),
        P(),
        P(),
        P(),
        P(),
        P(),
    )
    return jax.shard_map(
        shards, mesh=mesh, in_specs=placed, out_specs=(P("tiles", "swath"), P()), check_vma=False
    )
```

```python
import jax
import jax.numpy as jnp
import numpy as np
from jax import lax
from jax.experimental import pallas as pl
from jax.experimental.pallas import tpu as pltpu
from jax.sharding import PartitionSpec as P

TR = 512
BR = 128
RADIUS = 7
NBANDS = 6
CH = 16
NX = 4
NZ = 4
NY = 4
LANES = 128
HALO = 16
WIN = TR + 2 * HALO
ACC = WIN + 2 * HALO
QROWS = TR // NY
RQ = QROWS + 2 * HALO
COLS = NY * LANES
GROUPS = RQ // 8
KROWS = CH * 8 + 2 * CH
STRIP = 64
STEPS = 6
STRIPS = TR // STRIP

prior_weight = 0.5
ridge_term = 1.0
f32 = jnp.float32
bf16 = jnp.bfloat16
VMEM = pl.BlockSpec(memory_space=pltpu.VMEM)
SMEM = pl.BlockSpec(memory_space=pltpu.SMEM)
ANY = pl.BlockSpec(memory_space=pl.ANY)


def tile_id(x, z, c):
    return (x * NZ + z) * 2 + c


def along_y(k):
    return [(i, (i + k) % NY) for i in range(NY)]


def along_x(k):
    return [
        (tile_id(x, z, c), tile_id((x + k) % NX, z, c))
        for x in range(NX)
        for z in range(NZ)
        for c in range(2)
    ]


def along_z(k):
    return [
        (tile_id(x, z, c), tile_id(x, (z + k) % NZ, c))
        for x in range(NX)
        for z in range(NZ)
        for c in range(2)
    ]


core_pair = [(i, i ^ 1) for i in range(2 * NX * NZ)]


def call(kernel, outs, ins, scratch=(), flops=0, nbytes=0, name=None, grid=(), place=VMEM, alias={}):
    return pl.pallas_call(
        kernel,
        grid=grid,
        out_shape=outs,
        in_specs=ins,
        out_specs=place
        if isinstance(place, tuple)
        else jax.tree.map(lambda o: SMEM if o.shape == (NBANDS + 1,) else place, outs),
        scratch_shapes=list(scratch),
        input_output_aliases=alias,
        compiler_params=pltpu.CompilerParams(vmem_limit_bytes=56 * 1024 * 1024),
        cost_estimate=pl.CostEstimate(flops=flops, bytes_accessed=nbytes, transcendentals=0),
        name=name,
    )


def sds(shape, dtype):
    return jax.ShapeDtypeStruct(shape, dtype)


def add_blocks(meta, info, count, arrivals, add):
    c = info[2]
    for piece in range(8):
        arrivals[piece].wait()

        def body(j, carry, piece=piece):
            code = meta[piece, j]
            tile = code >> 9
            off = code & (TR - 1)
            mine = (tile & 1) == c

            @pl.when(mine)
            def _():
                add(piece, j, tile >> 1, off + 2 * HALO, 0, BR)

            @pl.when(jnp.logical_not(mine) & ((off > TR - BR - HALO) | (off < HALO)))
            def _():
                @pl.when((off > TR - BR - HALO) & (tile < 2 * NX * NZ - 1))
                def _():
                    add(piece, j, (tile + 1) >> 1, off - (TR - BR - HALO), BR - HALO, HALO)

                @pl.when((off < HALO) & (tile > 0))
                def _():
                    add(piece, j, (tile - 1) >> 1, off + 2 * HALO + TR, 0, HALO)

            return carry

        lax.fori_loop(0, count, body, 0, unroll=2)


def pack_kernel(info, dest, offset, temp, qual, *outs):
    s = info[3]
    count = temp.shape[0]
    lane = lax.broadcasted_iota(jnp.int32, (HALO, LANES), 1)
    row = lax.broadcasted_iota(jnp.int32, (HALO, LANES), 0)
    places = jnp.zeros((HALO, LANES), jnp.int32)
    for j in range(count):
        numbers = (dest[j], offset[j] >> 4, offset[j] & 15)
        for i, number in enumerate(numbers):
            places = jnp.where((lane == j) & (row == i), number, places)
    places = places.astype(f32).astype(bf16)
    for k, out in enumerate(outs):
        lanes = pl.ds(pl.multiple_of(lax.rem(s + k, NY) * LANES, LANES), LANES)
        for j in range(count):
            out[BR * j : BR * (j + 1), :] = qual[j, :, lanes]
            out[BR * (count + j) : BR * (count + j + 1), :] = temp[j, :, lanes]
        out[2 * count * BR :, :] = places

def scatter_kernel(info, *refs):
    pieces, outs = refs[0:8], refs[9:17]
    acc_n, acc_d, places, meta, sem, held, numbers, staged, in_sems, place_sems, out_sems = refs[17:]
    x, z = info[0], info[1]
    count = (pieces[0].shape[0] - HALO) // (2 * BR)
    small, large = [], []
    for i, piece in enumerate(pieces):
        tail = piece.at[pl.ds(2 * count * BR, HALO)]
        small.append(pltpu.make_async_copy(tail, numbers.at[i], place_sems.at[i]))
        small[i].start()
    for i, piece in enumerate(pieces):
        body = piece.at[pl.ds(0, 2 * count * BR)]
        large.append(pltpu.make_async_copy(body, held.at[i], in_sems.at[i]))
        large[i].start()
    for i in range(8):
        small[i].wait()
        number = numbers[i].astype(f32)
        code = number[0:1] * TR + number[1:2] * 16.0 + number[2:3]
        places[i : i + 1, :] = code.astype(jnp.int32)
    copy = pltpu.make_async_copy(places, meta, sem)
    copy.start()

    def clear(i, carry):
        acc_n[i] = jnp.zeros((ACC, LANES), f32)
        acc_d[i] = jnp.zeros((ACC, LANES), f32)
        return carry

    def add(piece, j, slot, start, row, rows):
        span = pl.ds(start, rows)
        at = pl.multiple_of(j * BR + row, HALO)
        q = held[piece, pl.ds(at, rows), :].astype(f32)
        t = held[piece, pl.ds(count * BR + at, rows), :].astype(f32)
        acc_d[slot, span, :] = acc_d[slot, span, :] + q
        acc_n[slot, span, :] = acc_n[slot, span, :] + q * t

    lax.fori_loop(0, NX * NZ, clear, 0)
    copy.wait()
    add_blocks(meta, info, count, large, add)
    leaving = []
    for kx in range(NX):
        for kz in range(NZ):
            slot = lax.rem(x + kx, NX) * NZ + lax.rem(z + kz, NZ)
            targets = (outs[kx].at[kz], outs[NX + kz].at[kx])
            for acc, target in zip((acc_n, acc_d), targets):
                i = len(leaving)
                staged[i] = acc[slot, HALO : HALO + WIN, :].astype(bf16)
                leaving.append(pltpu.make_async_copy(staged.at[i], target, out_sems.at[i]))
                leaving[i].start()
    for copy in leaving:
        copy.wait()


def scatter_scratch(rows):
    return [pltpu.VMEM((NX * NZ, ACC, LANES), f32)] * 2 + [
        pltpu.VMEM((8, LANES), jnp.int32),
        pltpu.SMEM((8, LANES), jnp.int32),
        pltpu.SemaphoreType.DMA,
        pltpu.VMEM((8, rows, LANES), bf16),
        pltpu.VMEM((8, HALO, LANES), bf16),
        pltpu.VMEM((2 * NX * NZ, WIN, LANES), bf16),
        pltpu.SemaphoreType.DMA((8,)),
        pltpu.SemaphoreType.DMA((8,)),
        pltpu.SemaphoreType.DMA((2 * NX * NZ,)),
    ]


def sum_kernel(a, b, c, d, *refs):
    for k, out in enumerate(refs[-4:]):
        out[...] = (a[k].astype(f32) + b[k].astype(f32)) + (c[k].astype(f32) + d[k].astype(f32))


def order_kernel(*refs):
    pass


def slab_kernel(reflect, land, first, last):
    lane = lax.broadcasted_iota(jnp.int32, (STRIP, LANES), 1)

    for plane in range(NBANDS + 1):
        sides = [jnp.zeros((STRIP, LANES), f32) for _ in range(2)]
        for i in range(STRIPS):
            rows = slice(STRIP * i, STRIP * (i + 1))
            cells = (reflect[plane, rows, :] if plane < NBANDS else land[rows, :]).astype(f32)
            for side, source in enumerate((0, LANES - HALO)):
                moved = pltpu.roll(cells, (HALO * i - source) % LANES, 1)
                sides[side] = jnp.where(lane >> 4 == i, moved, sides[side])
        first[plane] = sides[0].astype(bf16)
        last[plane] = sides[1].astype(bf16)


def beside_of(left, right, i):
    lane = lax.broadcasted_iota(jnp.int32, left.shape, 1)
    after = pltpu.roll(right, (-HALO * i) % LANES, 1)
    before = pltpu.roll(left, (HALO - HALO * i) % LANES, 1)
    return jnp.where(lane < HALO, after, jnp.where(lane < 2 * HALO, before, 0.0)).astype(bf16)


def edges_kernel(r0, r1, l0, l1, b0, b1, left, right, top, bottom):
    own = slice(0, LANES)
    sides = ((top, r0, l0, b0, 0, 0), (bottom, r1, l1, b1, STRIPS - 1, STRIP - HALO))
    for out, reflect, land, background, strip, row in sides:
        out[0:NBANDS, :, own] = reflect[...]
        out[NBANDS, :, own] = land[...].astype(f32).astype(bf16)
        high, low = split(background[...])
        out[NBANDS + 1, :, own] = high
        out[NBANDS + 2, :, own] = low
        for plane in range(NBANDS + 1):
            rows = slice(row, row + HALO)
            out[plane, :, LANES:] = beside_of(
                left[plane, rows, :].astype(f32), right[plane, rows, :].astype(f32), strip
            )
        for plane in range(NBANDS + 1, NBANDS + 3):
            out[plane, :, LANES:] = jnp.zeros((HALO, LANES), bf16)


def adjoint_kernel(
    reflect, land, above, below, left, right, row_h, row_l, col_h, col_l,
    adjoint, normal, window, beside, bands,
):
    for rows, edge in ((slice(0, HALO), above), (slice(HALO + TR, WIN), below)):
        window[:, rows, :] = edge[0 : NBANDS + 1, :, 0:LANES]
        beside[:, rows, :] = edge[0 : NBANDS + 1, :, LANES:]
    window[0:NBANDS, HALO : HALO + TR, :] = reflect[...]
    window[NBANDS, HALO : HALO + TR, :] = land[...].astype(f32).astype(bf16)

    def spread(plane, carry):
        before = left[plane].astype(f32)
        after = right[plane].astype(f32)
        for i in range(STRIPS):
            rows = slice(HALO + STRIP * i, HALO + STRIP * (i + 1))
            beside[plane, rows, :] = beside_of(before, after, i)
        return carry

    lax.fori_loop(0, NBANDS + 1, spread, 0)
    pairs = [(i, j) for i in range(NBANDS + 1) for j in range(i, NBANDS + 1)]
    own = slice(HALO, HALO + QROWS)

    def quarter(q, sums):
        rows = pl.ds(pl.multiple_of(QROWS * q, QROWS), RQ)

        def cells(plane):
            return jnp.concatenate([window[plane, rows, :], beside[plane, rows, :]], axis=1)

        land = cells(NBANDS).astype(f32)
        for band in range(NBANDS):
            x = cells(band)
            down = split(dot(row_h[...], x) + dot(row_l[...], x))
            bands[band] = dot3(down, (col_h[...], col_l[...]))
        for i in range(NBANDS + 1):
            value = split(land if i == 0 else land * bands[i - 1])
            down = split(dot3((row_h[own, :], row_l[own, :]), value))
            adjoint[i, pl.ds(pl.multiple_of(QROWS * q, QROWS), QROWS), :] = dot3(
                down, (col_h[:, 0:LANES], col_l[:, 0:LANES])
            )

        def step(g, sums):
            at = pl.multiple_of(HALO + 16 * g, 16)
            part = pl.ds(at, 16)
            mask = window[NBANDS, pl.ds(pl.multiple_of(QROWS * q + at, 16), 16), :].astype(f32)
            x = [None] + [bands[band, part, 0:LANES] for band in range(NBANDS)]
            mx = [mask] + [mask * x[i] for i in range(1, NBANDS + 1)]
            new = []
            for (i, j), total in zip(pairs, sums):
                v = mx[j] if i == 0 else mx[i] * x[j]
                new.append(total + (v[0:8] + v[8:16]))
            return tuple(new)

        return lax.fori_loop(0, QROWS // 16, step, sums)

    sums = lax.fori_loop(0, NY, quarter, tuple(jnp.zeros((8, LANES), f32) for _ in pairs))
    row = lax.broadcasted_iota(jnp.int32, (8, LANES), 0)
    lane = lax.broadcasted_iota(jnp.int32, (8, LANES), 1)
    result = jnp.zeros((8, LANES), f32)
    for (i, j), total in zip(pairs, sums):
        here = ((row == i) & (lane == j)) | ((row == j) & (lane == i))
        result = jnp.where(here, jnp.sum(total), result)
    normal[...] = result


def cut_kernel(window, after, out):
    for k in range(NY):
        out[k] = window[:, QROWS * k : QROWS * k + RQ, :]


def blend_kernel(info, *refs):
    nums, dens = refs[0:4], refs[4:8]
    background, above, below = refs[8:11]
    adjoint, normal = refs[11], refs[12]
    outs, field = refs[13:17], refs[17]
    first, last, s = info[4], info[5], info[3]
    num = nums[0][...].astype(f32)
    den = dens[0][...].astype(f32)
    for n in nums[1:]:
        num = num + n[...].astype(f32)
    for d in dens[1:]:
        den = den + d[...].astype(f32)
    ends = [
        edge[NBANDS + 1, :, 0:LANES].astype(f32) + edge[NBANDS + 2, :, 0:LANES].astype(f32) for edge in (above, below)
    ]
    prior = jnp.concatenate([ends[0], background[...], ends[1]], axis=0)
    row = lax.broadcasted_iota(jnp.int32, (WIN, LANES), 0)
    inside = (row >= HALO * first) & (row < WIN - HALO * last)
    blended = (prior_weight * prior + num) / (prior_weight + den)
    field[...] = jnp.where(inside, blended, 0.0)
    totals = [jnp.zeros((8, LANES), f32) for _ in range(NBANDS + 1)]

    def step(g, totals):
        cells = field[pl.ds(pl.multiple_of(HALO + 16 * g, 16), 16), :]
        rows = pl.ds(pl.multiple_of(16 * g, 16), 16)
        new = []
        for i, total in enumerate(totals):
            v = cells * adjoint[i, rows, :]
            new.append(total + (v[0:8] + v[8:16]))
        return tuple(new)

    totals = lax.fori_loop(0, TR // 16, step, tuple(totals))
    row = lax.broadcasted_iota(jnp.int32, (8, LANES), 0)
    lane = lax.broadcasted_iota(jnp.int32, (8, LANES), 1)
    sums = normal[...]
    for i, total in enumerate(totals):
        sums = jnp.where((row == i) & (lane == NBANDS + 1), jnp.sum(total), sums)
    for k, out in enumerate(outs):
        start = pl.multiple_of(lax.rem(s + k, NY) * QROWS, QROWS)
        out[0:RQ, :] = field[pl.ds(start, RQ), :]
        out[RQ:, :] = sums


def merge_kernel(b0, b1, b2, b3, out):
    total = (b0[...] + b2[...]) + (b1[...] + b3[...])
    out[...] = jnp.broadcast_to(total[None], out.shape)


def lane_place(s, k):
    return pl.ds(pl.multiple_of(lax.rem(s + NY - k, NY) * LANES, LANES), LANES)


def split(v):
    high = v.astype(bf16)
    return high, (v - high.astype(f32)).astype(bf16)


def dot(a, b):
    return jnp.dot(a, b, preferred_element_type=f32)


def dot3(a, b):
    return dot(a[0], b[0]) + (dot(a[0], b[1]) + dot(a[1], b[0]))


def row_inside(info, rows):
    row = lax.broadcasted_iota(jnp.int32, (rows, 1), 0)
    return (row >= HALO * info[6]) & (row < rows - HALO * info[7])


def bands_kernel(info, pieces, row_h, row_l, col_h, col_l, turn, fields, coarse, raw):
    for k in range(NY):
        raw[:, :, LANES * k : LANES * (k + 1)] = pieces[k]
    inside = row_inside(info, RQ)
    for band in range(NBANDS + 1):
        cells = raw[band]
        fields[band] = dot(cells, turn[...]).astype(bf16)
        if band < NBANDS:
            down = split(dot(row_h[...], cells) + dot(row_l[...], cells))
            coarse[band] = jnp.where(inside, dot3(down, (col_h[...], col_l[...])), 0.0)


def write(slot, start, value):
    rows = slice(start, start + value.shape[0])
    lane = lax.broadcasted_iota(jnp.int32, (value.shape[0], LANES), 1)
    for t in range(NY):
        slot[t + 1, rows, :] = value[:, LANES * t : LANES * (t + 1)]
    before = pltpu.roll(value[:, 3 * LANES :], 1, 1)
    after = pltpu.roll(value[:, :LANES], LANES - 1, 1)
    slot[0, rows, :] = jnp.where(lane > 0, before, 0.0)
    slot[5, rows, :] = jnp.where(lane < LANES - 1, after, 0.0)


def put(slot, g, hidden):
    for t in range(6):
        part = slice(LANES * t, LANES * (t + 1))
        hidden[g, 0:128, part] = slot[t].astype(bf16)
        hidden[g + 1, 128:144, part] = slot[t, pl.ds(7, CH, stride=8), :].astype(bf16)
        hidden[g - 1, 144:160, part] = slot[t, pl.ds(0, CH, stride=8), :].astype(bf16)


def clear_ends(hidden):
    zero_rows = jnp.zeros((CH, 6 * LANES), bf16)
    hidden[1, 128:144, :] = zero_rows
    hidden[GROUPS - 2, 144:160, :] = zero_rows


def assemble_kernel(
    info, b0, b1, b2, b3, row_h, row_l, col_h, col_l, turn, fields_in, bands_in,
    coarse, hidden_out, natural, blended, group, fields, bands, hidden, in_sems, out_sems,
):
    s = info[3]
    arrays = ((fields_in, fields), (bands_in, bands))
    copies = [pltpu.make_async_copy(a, b, in_sems.at[i]) for i, (a, b) in enumerate(arrays)]
    for copy in copies:
        copy.start()
    for k, piece in enumerate((b0, b1, b2, b3)):
        natural[:, lane_place(s, k)] = piece[0:RQ, :]
    high, low = split(natural[...])
    down = split(dot3((row_h[...], row_l[...]), (high, low)))
    coarse[...] = jnp.where(
        row_inside(info, RQ), dot3(down, (col_h[...], col_l[...])), 0.0
    )
    blended[...] = dot(high, turn[...])
    clear_ends(hidden)
    for copy in copies:
        copy.wait()

    def leave(m):
        part = pl.ds(2 * m - 1, 2)
        return pltpu.make_async_copy(hidden.at[part], hidden_out.at[part], out_sems.at[m])

    def step(m, carry):
        rows = pl.ds(pl.multiple_of(16 * m, 16), 16)
        values = [jnp.zeros((16, COLS), f32), blended[rows, :], coarse[rows, :]]
        values.append(fields[NBANDS, rows, :].astype(f32))
        values += [fields[band, rows, :].astype(f32) for band in range(NBANDS)]
        values += [bands[band, rows, :] for band in range(NBANDS)]
        for half in range(2):
            g = 2 * m + half
            for channel, value in enumerate(values):
                write(group.at[half], 8 * channel, value[8 * half : 8 * half + 8])

            @pl.when((g >= 1) & (g <= GROUPS - 2))
            def _():
                put(group.at[half], g, hidden)

        @pl.when(m >= 1)
        def _():
            leave(m).start()

        return carry

    lax.fori_loop(0, GROUPS // 2, step, 0)
    for m in range(1, GROUPS // 2):
        leave(m).wait()


def assemble_scratch():
    return [
        pltpu.VMEM((RQ, COLS), f32),
        pltpu.VMEM((RQ, COLS), f32),
        pltpu.VMEM((2, 6, CH * 8, LANES), f32),
        pltpu.VMEM((NBANDS + 1, RQ, COLS), bf16),
        pltpu.VMEM((NBANDS, RQ, COLS), f32),
        pltpu.VMEM((GROUPS, KROWS, 6 * LANES), bf16),
        pltpu.SemaphoreType.DMA((2,)),
        pltpu.SemaphoreType.DMA((GROUPS // 2,)),
    ]


def solve(sums):
    row = lax.broadcasted_iota(jnp.int32, (8, LANES), 0)
    lane = lax.broadcasted_iota(jnp.int32, (8, LANES), 1)
    work = sums + jnp.where((row == lane) & (row <= NBANDS), ridge_term, 0.0)
    for pivot in range(NBANDS + 1):
        pivot_row = work[pivot : pivot + 1, :]
        pivot_value = jnp.sum(jnp.where(lane[0:1] == pivot, pivot_row, 0.0), axis=1, keepdims=True)
        scaled = pivot_row / pivot_value
        factor = jnp.sum(jnp.where(lane == pivot, work, 0.0), axis=1, keepdims=True)
        work = jnp.where(row == pivot, scaled, work - factor * scaled)
    picked = jnp.where(lane == NBANDS + 1, work, 0.0)
    return [jnp.sum(picked[i : i + 1, :]) for i in range(NBANDS + 1)]


def main_kernel(
    info, head, sums, coarse_in, fields_in, bands_in, kernels, biases, turn_back_in, stacked_in,
    o0, o1, o2, o3, fit_out, first_h, second_h, group, base, result,
    coarse, fields, bands, turn_back, stacked, sems, stack_sems,
):
    s = info[3]
    arrays = ((coarse_in, coarse), (fields_in, fields), (bands_in, bands))
    copies = [pltpu.make_async_copy(a, b, sems.at[i]) for i, (a, b) in enumerate(arrays)]
    for copy in copies:
        copy.start()
    steps = STEPS

    def stack_copy(i):
        part = pl.ds(1 + steps * i, steps)
        return pltpu.make_async_copy(stacked_in.at[part], stacked.at[part], stack_sems.at[i])

    for i in range((GROUPS - 2) // steps):
        stack_copy(i).start()
    turn_copy = pltpu.make_async_copy(turn_back_in, turn_back, sems.at[3])
    turn_copy.start()
    coefs = solve(jnp.sum(sums[...], axis=0))
    for i in range(NBANDS + 1):
        fit_out[i] = coefs[i]
    for copy in copies:
        copy.wait()
    clear_ends(first_h)
    clear_ends(second_h)

    def start(m, carry):
        rows = pl.ds(pl.multiple_of(16 * m, 16), 16)
        value = coarse[rows, :]
        for band in range(NBANDS):
            value = value + coefs[band + 1] * (
                fields[band, rows, :].astype(f32) - bands[band, rows, :]
            )
        lane = lax.broadcasted_iota(jnp.int32, (16, LANES), 1)
        base[rows, LANES : 5 * LANES] = value
        base[rows, 0:LANES] = jnp.where(lane > 0, pltpu.roll(value[:, 3 * LANES :], 1, 1), 0.0)
        base[rows, 5 * LANES :] = jnp.where(
            lane < LANES - 1, pltpu.roll(value[:, :LANES], LANES - 1, 1), 0.0
        )
        return carry

    lax.fori_loop(0, GROUPS // 2, start, 0)
    edge_row = lax.broadcasted_iota(jnp.int32, (CH, 6 * LANES), 0) == 0

    def with_base(g):
        own = stacked[g, 0:16, :].astype(f32)
        at = pl.multiple_of(8 * g, 8)
        own = jnp.concatenate([base[pl.ds(at, 8), :], own[8:16]], axis=0).astype(bf16)
        above = jnp.where(
            edge_row, base[pl.ds(8 * g - 1, 1), :], stacked[g, 128:144, :].astype(f32)
        )
        below = jnp.where(
            edge_row, base[pl.ds(8 * g + 8, 1), :], stacked[g, 144:160, :].astype(f32)
        )
        return jnp.concatenate(
            [own, stacked[g, 16:128, :], above.astype(bf16), below.astype(bf16)], axis=0
        )

    def convolved(layer, cells):
        spans = [slice(LANES * b, LANES * (b + 4)) for b in range(3)]
        taps = jnp.concatenate(
            [cells[0:128, span] for span in spans] + [cells[128:160, span] for span in spans],
            axis=0,
        )
        bias = jnp.concatenate([biases[layer]] * NY, axis=1)
        return jnp.maximum(dot(kernels[layer], taps) + bias, 0.0)

    for layer, following in enumerate((first_h, second_h)):

        def body(i, carry, layer=layer, following=following):
            if layer == 0:
                stack_copy(i).wait()
            for u in range(steps):
                g = 1 + steps * i + u
                cells = with_base(g) if layer == 0 else first_h[g]
                outside = ((g == 1) & (info[6] == 1)) | ((g == GROUPS - 2) & (info[7] == 1))
                keep = jnp.where(outside, 0.0, 1.0)
                write(group.at[u], 0, convolved(layer, cells) * keep)
                put(group.at[u], g, following)
            return carry

        lax.fori_loop(0, (GROUPS - 2) // steps, body, 0)

    def last(i, carry):
        mask = fields[NBANDS, pl.ds(pl.multiple_of(HALO + 32 * i, 32), 32), :].astype(f32)
        for u in range(4):
            g = 2 + 4 * i + u
            third = convolved(2, second_h[g]).astype(bf16).astype(f32)
            total = head[0] * third[0:8]
            for channel in range(1, CH):
                total = total + head[channel] * third[8 * channel : 8 * channel + 8]
            rows = pl.ds(pl.multiple_of(8 * g, 8), 8)
            out_rows = pl.ds(pl.multiple_of(8 * g - HALO, 8), 8)
            result[out_rows, :] = (
                base[rows, LANES : 5 * LANES] + mask[8 * u : 8 * u + 8] * total
            )
        return carry

    lax.fori_loop(0, QROWS // 32, last, 0)
    turn_copy.wait()
    high, low = split(result[...])
    result[...] = dot(high, turn_back[...]) + dot(low, turn_back[...])
    for k, out in enumerate((o0, o1, o2, o3)):
        out[...] = result[:, pl.ds(pl.multiple_of(lax.rem(s + k, NY) * LANES, LANES), LANES)]


def main_scratch():
    hidden = pltpu.VMEM((GROUPS, KROWS, 6 * LANES), bf16)
    return [
        hidden,
        hidden,
        pltpu.VMEM((STEPS, 6, CH * 8, LANES), f32),
        pltpu.VMEM((RQ, 6 * LANES), f32),
        pltpu.VMEM((QROWS, COLS), f32),
        pltpu.VMEM((RQ, COLS), f32),
        pltpu.VMEM((NBANDS + 1, RQ, COLS), bf16),
        pltpu.VMEM((NBANDS, RQ, COLS), f32),
        pltpu.VMEM((COLS, COLS), bf16),
        hidden,
        pltpu.SemaphoreType.DMA((4,)),
        pltpu.SemaphoreType.DMA(((GROUPS - 2) // STEPS,)),
    ]


def join_kernel(info, o0, o1, o2, o3, out):
    s = info[3]
    for k, piece in enumerate((o0, o1, o2, o3)):
        start = pl.multiple_of(lax.rem(s + NY - k, NY) * QROWS, QROWS)
        out[pl.ds(start, QROWS), :] = piece[...]


def band_matrix(rows, columns):
    offsets = np.arange(2 * RADIUS + 1) - RADIUS
    norm = np.sum(np.exp(-0.125 * offsets**2))
    apart = rows[:, None] - columns[None, :]
    weights = np.where(np.abs(apart) <= RADIUS, np.exp(-0.125 * apart**2) / norm, 0.0)
    high = weights.astype(bf16)
    return jnp.asarray(high), jnp.asarray((weights - high.astype(np.float64)).astype(bf16))


def matrices_kernel(taps, bias, kernels, biases):
    def iota(size, axis):
        return lax.broadcasted_iota(jnp.int32, (size, size), axis)

    tall = (CH * 8, CH)
    spread_rows = (
        lax.broadcasted_iota(jnp.int32, tall, 0) >> 3 == lax.broadcasted_iota(jnp.int32, tall, 1)
    )
    spread_rows = jnp.where(spread_rows, 1.0, 0.0).astype(bf16)
    wide = (CH, CH * 8)
    channel, lane = (lax.broadcasted_iota(jnp.int32, wide, a) for a in range(2))
    spread_lanes = jnp.where(lane >> 3 == channel, 1.0, 0.0).astype(bf16)
    r, l = iota(CH * 8, 0), iota(CH * 8, 1)
    up = (l & 7) - (r & 7)
    for layer in range(3):
        halo = jnp.zeros((CH * 8, CH * 8), f32)
        for b in range(3):
            own = jnp.zeros((CH * 8, CH * 8), f32)
            for a in range(3):
                column = dot(spread_rows, taps[layer, a, b]).astype(bf16)
                own = jnp.where(up == a - 1, dot(column, spread_lanes), own)
                if a == 1:
                    continue
                at = 32 * b + (0 if a == 0 else CH)
                placed = jnp.where(lane == channel + at, 1.0, 0.0).astype(bf16)
                halo = halo + jnp.where((r & 7) == (0 if a == 0 else 7), dot(column, placed), 0.0)
            kernels[layer, :, 128 * b : 128 * b + 128] = own.astype(bf16)
        kernels[layer, :, 384:480] = halo[:, 0:96].astype(bf16)
        for o in range(CH):
            biases[layer, 8 * o : 8 * o + 8, :] = jnp.broadcast_to(
                bias[CH * layer + o : CH * layer + o + 1, :], (8, LANES)
            )


def exchange(pieces, axis, route):
    return [pieces[0]] + [lax.ppermute(pieces[k], axis, route(k)) for k in range(1, 4)]


def shards(
    blk_temp, blk_qual, dest_tile, blk_offset, background, reflect, land,
    conv_first, bias_first, conv_second, bias_second, conv_third, bias_third, head,
):
    tile = lax.axis_index("tiles")
    s = lax.axis_index("swath")
    tiles = lax.axis_size("tiles")
    x, z, c = tile // (2 * NZ), (tile // 2) % NZ, tile % 2
    first = tile == 0
    last = tile == tiles - 1
    info = jnp.stack(
        [x, z, c, s, first, last, first & (s == 0), last & (s == NY - 1)]
    ).astype(jnp.int32)

    count = blk_temp.shape[0]
    down = [(i, i + 1) for i in range(tiles - 1)]
    up = [(i + 1, i) for i in range(tiles - 1)]

    def edge(last_rows):
        at = TR // HALO - 1 if last_rows else 0
        return [
            pl.BlockSpec((NBANDS, HALO, LANES), lambda i: (0, at, 0)),
            pl.BlockSpec((HALO, LANES), lambda i: (at, 0)),
            pl.BlockSpec((HALO, LANES), lambda i: (at, 0)),
        ]

    edges = [spec for pair in zip(edge(False), edge(True)) for spec in pair]
    row_h, row_l = band_matrix(np.arange(RQ), np.arange(RQ))
    natural = np.arange(COLS)
    place = NY * (natural % LANES) + natural // LANES
    col_h, col_l = band_matrix(natural, place)
    turn = jnp.asarray((natural[:, None] == place[None, :]).astype(bf16))
    turn_back = jnp.asarray((place[:, None] == natural[None, :]).astype(bf16))
    lanes = np.arange(2 * LANES)
    spot = np.where(lanes < LANES + HALO, lanes, lanes - LANES - 2 * HALO)
    spot = np.where(lanes < LANES + 2 * HALO, spot, 1000 * lanes)
    near_h, near_l = band_matrix(spot, spot)

    strip = sds((NBANDS + 1, STRIP, LANES), bf16)
    first_columns, last_columns = call(slab_kernel, (strip, strip), [VMEM] * 2, name="slab")(
        reflect, land
    )
    from_left = lax.ppermute(last_columns, "swath", [(i, i + 1) for i in range(NY - 1)])
    from_right = lax.ppermute(first_columns, "swath", [(i + 1, i) for i in range(NY - 1)])
    packed = call(
        pack_kernel,
        (sds((2 * count * BR + HALO, LANES), bf16),) * 4,
        [SMEM] * 3 + [VMEM] * 2,
        name="pack",
    )(info, dest_tile, blk_offset, blk_temp, blk_qual)
    block = sds(packed[0].shape, bf16)
    packed = tuple(packed[0:1]) + tuple(call(
        order_kernel, (block,) * 3, [ANY] * 5, place=ANY, alias={0: 0, 1: 1, 2: 2}, name="order"
    )(*packed[1:], from_left, from_right))
    edge_rows = sds((NBANDS + 3, HALO, 2 * LANES), bf16)
    top, bottom = call(
        edges_kernel, (edge_rows,) * 2, edges + [VMEM] * 2, grid=(1,), name="edges"
    )(reflect, reflect, land, land, background, background, from_left, from_right)
    above = lax.ppermute(bottom, "tiles", down)
    below = lax.ppermute(top, "tiles", up)

    adjoint, normal, window = call(
        adjoint_kernel,
        (
            sds((NBANDS + 1, TR, LANES), f32),
            sds((8, LANES), f32),
            sds((NBANDS + 1, WIN, LANES), bf16),
        ),
        [VMEM] * 10,
        scratch=[
            pltpu.VMEM((NBANDS + 1, WIN, LANES), bf16),
            pltpu.VMEM((NBANDS, RQ, 2 * LANES), f32),
        ],
        name="adjoint",
    )(reflect, land, above, below, from_left, from_right, row_h, row_l, near_h, near_l)
    taps = jnp.transpose(jnp.stack([conv_first, conv_second, conv_third]), (0, 3, 4, 1, 2))
    bias = jnp.concatenate([bias_first, bias_second, bias_third])
    kernels, biases = call(
        matrices_kernel,
        (sds((3, CH * 8, 3 * KROWS), bf16), sds((3, CH * 8, LANES), f32)),
        [VMEM] * 2,
        name="matrices",
    )(taps, jnp.broadcast_to(bias[:, None], (3 * CH, LANES)))
    weights = head.astype(f32)

    chip = exchange(packed, "swath", along_y)
    chip[1] = call(
        order_kernel, (block,), [ANY] * 3, place=ANY, alias={0: 0}, name="order"
    )(chip[1], adjoint, kernels)[0]
    cut = call(
        cut_kernel,
        sds((NY, NBANDS + 1, RQ, LANES), bf16),
        [VMEM] + [ANY],
        name="cut",
    )(window, chip[2])
    pieces = lax.all_to_all(cut, "swath", split_axis=0, concat_axis=0, tiled=True)
    fields, bands = call(
        bands_kernel,
        (sds((NBANDS + 1, RQ, COLS), bf16), sds((NBANDS, RQ, COLS), f32)),
        [SMEM] + [VMEM] * 6,
        scratch=[pltpu.VMEM((NBANDS + 1, RQ, COLS), bf16)],
        flops=2 * 6 * 160 * 512 * (320 + 1536),
        nbytes=10 << 20,
        name="bands",
    )(info, pieces, row_h, row_l, col_h, col_l, turn)
    chip[2] = call(
        order_kernel, (block,), [ANY] * 2, place=ANY, alias={0: 0}, name="order"
    )(chip[2], cut)[0]
    chip = chip + [lax.ppermute(p, "tiles", core_pair) for p in chip]

    part = sds((4, WIN, LANES), bf16)
    routed = call(
        scatter_kernel,
        (part,) * 8,
        [SMEM] + [ANY] * 9,
        scratch=scatter_scratch(2 * count * BR),
        place=ANY,
        flops=96 * 128 * 128 * 8,
        nbytes=12 << 20,
        name="scatter",
    )(info, *chip, cut)
    nums = exchange(routed[0:4], "tiles", along_x)
    dens = exchange(routed[4:8], "tiles", along_z)

    one = sds((WIN, LANES), f32)
    summed = call(sum_kernel, (one,) * 4, [VMEM] * 4 + [ANY], nbytes=3 << 20, name="add")
    nums = summed(*nums, fields)
    dens = summed(*dens, fields)
    nums = exchange(nums, "tiles", along_z)
    dens = exchange(dens, "tiles", along_x)
    rows = call(
        blend_kernel,
        (sds((RQ + 8, LANES), f32),) * 4,
        [SMEM] + [VMEM] * 13,
        scratch=[pltpu.VMEM((WIN, LANES), f32)],
        nbytes=3 << 20,
        name="blend",
    )(info, *nums, *dens, background, above, below, adjoint, normal)
    rows = exchange(rows, "swath", along_y)
    sums = call(
        merge_kernel,
        sds((tiles, 8, LANES), f32),
        [pl.BlockSpec((8, LANES), lambda i: (RQ // 8, 0))] * 4,
        grid=(1,),
        name="merge",
    )(*rows)
    sums = lax.all_to_all(sums, "tiles", split_axis=0, concat_axis=0, tiled=True)
    coarse, stacked = call(
        assemble_kernel,
        (sds((RQ, COLS), f32), sds((GROUPS, KROWS, 6 * LANES), bf16)),
        [SMEM] + [VMEM] * 9 + [ANY] * 2,
        scratch=assemble_scratch(),
        place=(VMEM, ANY),
        flops=2 * 160 * 512 * (480 + 1536),
        nbytes=8 << 20,
        name="assemble",
    )(info, *rows, row_h, row_l, col_h, col_l, turn, fields, bands)
    *sharp, fit_coefs = call(
        main_kernel,
        (sds((QROWS, LANES), f32),) * 4 + (sds((NBANDS + 1,), f32),),
        [SMEM, SMEM, VMEM] + [ANY] * 3 + [VMEM] * 2 + [ANY] * 2,
        scratch=main_scratch(),
        flops=3 * 18 * 2 * 384 * 160 * 512,
        nbytes=8 << 20,
        name="convolve",
    )(info, weights, sums, coarse, fields, bands, kernels, biases, turn_back, stacked)
    sharp = exchange(sharp, "swath", along_y)
    out = call(join_kernel, sds((TR, LANES), f32), [SMEM] + [VMEM] * 4, name="join")(info, *sharp)
    return out, fit_coefs


def solution(mesh):
    placed = (
        P(("tiles", "swath"), None, None),
        P(("tiles", "swath"), None, None),
        P(("tiles", "swath")),
        P(("tiles", "swath")),
        P("tiles", "swath"),
        P(None, "tiles", "swath"),
        P("tiles", "swath"),
        P(),
        P(),
        P(),
        P(),
        P(),
        P(),
        P(),
    )
    return jax.shard_map(
        shards, mesh=mesh, in_specs=placed, out_specs=(P("tiles", "swath"), P()), check_vma=False
    )
```

```python
import jax
import jax.numpy as jnp
import numpy as np
from jax import lax
from jax.experimental import pallas as pl
from jax.experimental.pallas import tpu as pltpu
from jax.sharding import PartitionSpec as P

TR = 512
BR = 128
RADIUS = 7
NBANDS = 6
CH = 16
NX = 4
NZ = 4
NY = 4
LANES = 128
HALO = 16
WIN = TR + 2 * HALO
ACC = WIN + 2 * HALO
QROWS = TR // NY
RQ = QROWS + 2 * HALO
COLS = NY * LANES
GROUPS = RQ // 8
KROWS = CH * 8 + 2 * CH
STRIP = 64
STEPS = 6
STRIPS = TR // STRIP

prior_weight = 0.5
ridge_term = 1.0
f32 = jnp.float32
bf16 = jnp.bfloat16
VMEM = pl.BlockSpec(memory_space=pltpu.VMEM)
SMEM = pl.BlockSpec(memory_space=pltpu.SMEM)
ANY = pl.BlockSpec(memory_space=pl.ANY)


def tile_id(x, z, c):
    return (x * NZ + z) * 2 + c


def along_y(k):
    return [(i, (i + k) % NY) for i in range(NY)]


def along_x(k):
    return [
        (tile_id(x, z, c), tile_id((x + k) % NX, z, c))
        for x in range(NX)
        for z in range(NZ)
        for c in range(2)
    ]


def along_z(k):
    return [
        (tile_id(x, z, c), tile_id(x, (z + k) % NZ, c))
        for x in range(NX)
        for z in range(NZ)
        for c in range(2)
    ]


core_pair = [(i, i ^ 1) for i in range(2 * NX * NZ)]


def call(kernel, outs, ins, scratch=(), flops=0, nbytes=0, name=None, grid=(), place=VMEM, alias={}):
    return pl.pallas_call(
        kernel,
        grid=grid,
        out_shape=outs,
        in_specs=ins,
        out_specs=place
        if isinstance(place, tuple)
        else jax.tree.map(lambda o: SMEM if o.shape == (NBANDS + 1,) else place, outs),
        scratch_shapes=list(scratch),
        input_output_aliases=alias,
        compiler_params=pltpu.CompilerParams(vmem_limit_bytes=56 * 1024 * 1024),
        cost_estimate=pl.CostEstimate(flops=flops, bytes_accessed=nbytes, transcendentals=0),
        name=name,
    )


def sds(shape, dtype):
    return jax.ShapeDtypeStruct(shape, dtype)


def add_blocks(meta, info, count, arrivals, add):
    c = info[2]
    for piece in range(8):
        arrivals[piece].wait()

        def body(j, carry, piece=piece):
            code = meta[piece, j]
            tile = code >> 9
            off = code & (TR - 1)
            mine = (tile & 1) == c

            @pl.when(mine)
            def _():
                add(piece, j, tile >> 1, off + 2 * HALO, 0, BR)

            @pl.when(jnp.logical_not(mine) & ((off > TR - BR - HALO) | (off < HALO)))
            def _():
                @pl.when((off > TR - BR - HALO) & (tile < 2 * NX * NZ - 1))
                def _():
                    add(piece, j, (tile + 1) >> 1, off - (TR - BR - HALO), BR - HALO, HALO)

                @pl.when((off < HALO) & (tile > 0))
                def _():
                    add(piece, j, (tile - 1) >> 1, off + 2 * HALO + TR, 0, HALO)

            return carry

        lax.fori_loop(0, count, body, 0, unroll=4)


def pack_kernel(info, dest, offset, temp, qual, *outs):
    s = info[3]
    count = temp.shape[0]
    lane = lax.broadcasted_iota(jnp.int32, (HALO, LANES), 1)
    row = lax.broadcasted_iota(jnp.int32, (HALO, LANES), 0)
    places = jnp.zeros((HALO, LANES), jnp.int32)
    for j in range(count):
        numbers = (dest[j], offset[j] >> 4, offset[j] & 15)
        for i, number in enumerate(numbers):
            places = jnp.where((lane == j) & (row == i), number, places)
    places = places.astype(f32).astype(bf16)
    for k, out in enumerate(outs):
        lanes = pl.ds(pl.multiple_of(lax.rem(s + k, NY) * LANES, LANES), LANES)
        for j in range(count):
            out[BR * j : BR * (j + 1), :] = qual[j, :, lanes]
            out[BR * (count + j) : BR * (count + j + 1), :] = temp[j, :, lanes]
        out[2 * count * BR :, :] = places

def scatter_kernel(info, *refs):
    pieces, outs = refs[0:8], refs[9:17]
    acc_n, acc_d, places, meta, sem, held, numbers, staged, in_sems, place_sems, out_sems = refs[17:]
    x, z = info[0], info[1]
    count = (pieces[0].shape[0] - HALO) // (2 * BR)
    small, large = [], []
    for i, piece in enumerate(pieces):
        tail = piece.at[pl.ds(2 * count * BR, HALO)]
        small.append(pltpu.make_async_copy(tail, numbers.at[i], place_sems.at[i]))
        small[i].start()
    for i, piece in enumerate(pieces):
        body = piece.at[pl.ds(0, 2 * count * BR)]
        large.append(pltpu.make_async_copy(body, held.at[i], in_sems.at[i]))
        large[i].start()
    for i in range(8):
        small[i].wait()
        number = numbers[i].astype(f32)
        code = number[0:1] * TR + number[1:2] * 16.0 + number[2:3]
        places[i : i + 1, :] = code.astype(jnp.int32)
    copy = pltpu.make_async_copy(places, meta, sem)
    copy.start()

    def clear(i, carry):
        acc_n[i] = jnp.zeros((ACC, LANES), f32)
        acc_d[i] = jnp.zeros((ACC, LANES), f32)
        return carry

    def add(piece, j, slot, start, row, rows):
        span = pl.ds(start, rows)
        at = pl.multiple_of(j * BR + row, HALO)
        q = held[piece, pl.ds(at, rows), :].astype(f32)
        t = held[piece, pl.ds(count * BR + at, rows), :].astype(f32)
        acc_d[slot, span, :] = acc_d[slot, span, :] + q
        acc_n[slot, span, :] = acc_n[slot, span, :] + q * t

    lax.fori_loop(0, NX * NZ, clear, 0)
    copy.wait()
    add_blocks(meta, info, count, large, add)
    leaving = []
    for kx in range(NX):
        for kz in range(NZ):
            slot = lax.rem(x + kx, NX) * NZ + lax.rem(z + kz, NZ)
            targets = (outs[kx].at[kz], outs[NX + kz].at[kx])
            for acc, target in zip((acc_n, acc_d), targets):
                i = len(leaving)
                staged[i] = acc[slot, HALO : HALO + WIN, :].astype(bf16)
                leaving.append(pltpu.make_async_copy(staged.at[i], target, out_sems.at[i]))
                leaving[i].start()
    for copy in leaving:
        copy.wait()


def scatter_scratch(rows):
    return [pltpu.VMEM((NX * NZ, ACC, LANES), f32)] * 2 + [
        pltpu.VMEM((8, LANES), jnp.int32),
        pltpu.SMEM((8, LANES), jnp.int32),
        pltpu.SemaphoreType.DMA,
        pltpu.VMEM((8, rows, LANES), bf16),
        pltpu.VMEM((8, HALO, LANES), bf16),
        pltpu.VMEM((2 * NX * NZ, WIN, LANES), bf16),
        pltpu.SemaphoreType.DMA((8,)),
        pltpu.SemaphoreType.DMA((8,)),
        pltpu.SemaphoreType.DMA((2 * NX * NZ,)),
    ]


def sum_kernel(a, b, c, d, *refs):
    for k, out in enumerate(refs[-4:]):
        out[...] = (a[k].astype(f32) + b[k].astype(f32)) + (c[k].astype(f32) + d[k].astype(f32))


def order_kernel(*refs):
    pass


def slab_kernel(reflect, land, first, last):
    lane = lax.broadcasted_iota(jnp.int32, (STRIP, LANES), 1)

    for plane in range(NBANDS + 1):
        sides = [jnp.zeros((STRIP, LANES), f32) for _ in range(2)]
        for i in range(STRIPS):
            rows = slice(STRIP * i, STRIP * (i + 1))
            cells = (reflect[plane, rows, :] if plane < NBANDS else land[rows, :]).astype(f32)
            for side, source in enumerate((0, LANES - HALO)):
                moved = pltpu.roll(cells, (HALO * i - source) % LANES, 1)
                sides[side] = jnp.where(lane >> 4 == i, moved, sides[side])
        first[plane] = sides[0].astype(bf16)
        last[plane] = sides[1].astype(bf16)


def beside_of(left, right, i):
    lane = lax.broadcasted_iota(jnp.int32, left.shape, 1)
    after = pltpu.roll(right, (-HALO * i) % LANES, 1)
    before = pltpu.roll(left, (HALO - HALO * i) % LANES, 1)
    return jnp.where(lane < HALO, after, jnp.where(lane < 2 * HALO, before, 0.0)).astype(bf16)


def edges_kernel(r0, r1, l0, l1, b0, b1, left, right, top, bottom):
    own = slice(0, LANES)
    sides = ((top, r0, l0, b0, 0, 0), (bottom, r1, l1, b1, STRIPS - 1, STRIP - HALO))
    for out, reflect, land, background, strip, row in sides:
        out[0:NBANDS, :, own] = reflect[...]
        out[NBANDS, :, own] = land[...].astype(f32).astype(bf16)
        high, low = split(background[...])
        out[NBANDS + 1, :, own] = high
        out[NBANDS + 2, :, own] = low
        for plane in range(NBANDS + 1):
            rows = slice(row, row + HALO)
            out[plane, :, LANES:] = beside_of(
                left[plane, rows, :].astype(f32), right[plane, rows, :].astype(f32), strip
            )
        for plane in range(NBANDS + 1, NBANDS + 3):
            out[plane, :, LANES:] = jnp.zeros((HALO, LANES), bf16)


def adjoint_kernel(
    reflect, land, above, below, left, right, row_h, row_l, col_h, col_l,
    adjoint, normal, window, beside, bands,
):
    for rows, edge in ((slice(0, HALO), above), (slice(HALO + TR, WIN), below)):
        window[:, rows, :] = edge[0 : NBANDS + 1, :, 0:LANES]
        beside[:, rows, :] = edge[0 : NBANDS + 1, :, LANES:]
    window[0:NBANDS, HALO : HALO + TR, :] = reflect[...]
    window[NBANDS, HALO : HALO + TR, :] = land[...].astype(f32).astype(bf16)

    def spread(plane, carry):
        before = left[plane].astype(f32)
        after = right[plane].astype(f32)
        for i in range(STRIPS):
            rows = slice(HALO + STRIP * i, HALO + STRIP * (i + 1))
            beside[plane, rows, :] = beside_of(before, after, i)
        return carry

    lax.fori_loop(0, NBANDS + 1, spread, 0)
    pairs = [(i, j) for i in range(NBANDS + 1) for j in range(i, NBANDS + 1)]
    own = slice(HALO, HALO + QROWS)

    def quarter(q, sums):
        rows = pl.ds(pl.multiple_of(QROWS * q, QROWS), RQ)

        def cells(plane):
            return jnp.concatenate([window[plane, rows, :], beside[plane, rows, :]], axis=1)

        land = cells(NBANDS).astype(f32)
        for band in range(NBANDS):
            x = cells(band)
            down = split(dot(row_h[...], x) + dot(row_l[...], x))
            bands[band] = dot3(down, (col_h[...], col_l[...]))
        for i in range(NBANDS + 1):
            value = split(land if i == 0 else land * bands[i - 1])
            down = split(dot3((row_h[own, :], row_l[own, :]), value))
            adjoint[i, pl.ds(pl.multiple_of(QROWS * q, QROWS), QROWS), :] = dot3(
                down, (col_h[:, 0:LANES], col_l[:, 0:LANES])
            )

        def step(g, sums):
            at = pl.multiple_of(HALO + 16 * g, 16)
            part = pl.ds(at, 16)
            mask = window[NBANDS, pl.ds(pl.multiple_of(QROWS * q + at, 16), 16), :].astype(f32)
            x = [None] + [bands[band, part, 0:LANES] for band in range(NBANDS)]
            mx = [mask] + [mask * x[i] for i in range(1, NBANDS + 1)]
            new = []
            for (i, j), total in zip(pairs, sums):
                v = mx[j] if i == 0 else mx[i] * x[j]
                new.append(total + (v[0:8] + v[8:16]))
            return tuple(new)

        return lax.fori_loop(0, QROWS // 16, step, sums)

    sums = lax.fori_loop(0, NY, quarter, tuple(jnp.zeros((8, LANES), f32) for _ in pairs))
    row = lax.broadcasted_iota(jnp.int32, (8, LANES), 0)
    lane = lax.broadcasted_iota(jnp.int32, (8, LANES), 1)
    result = jnp.zeros((8, LANES), f32)
    for (i, j), total in zip(pairs, sums):
        here = ((row == i) & (lane == j)) | ((row == j) & (lane == i))
        result = jnp.where(here, jnp.sum(total), result)
    normal[...] = result


def cut_kernel(window, after, out):
    for k in range(NY):
        out[k] = window[:, QROWS * k : QROWS * k + RQ, :]


def blend_kernel(info, *refs):
    nums, dens = refs[0:4], refs[4:8]
    background, above, below = refs[8:11]
    adjoint, normal = refs[11], refs[12]
    outs, field = refs[13:17], refs[17]
    first, last, s = info[4], info[5], info[3]
    num = nums[0][...].astype(f32)
    den = dens[0][...].astype(f32)
    for n in nums[1:]:
        num = num + n[...].astype(f32)
    for d in dens[1:]:
        den = den + d[...].astype(f32)
    ends = [
        edge[NBANDS + 1, :, 0:LANES].astype(f32) + edge[NBANDS + 2, :, 0:LANES].astype(f32) for edge in (above, below)
    ]
    prior = jnp.concatenate([ends[0], background[...], ends[1]], axis=0)
    row = lax.broadcasted_iota(jnp.int32, (WIN, LANES), 0)
    inside = (row >= HALO * first) & (row < WIN - HALO * last)
    blended = (prior_weight * prior + num) / (prior_weight + den)
    field[...] = jnp.where(inside, blended, 0.0)
    totals = [jnp.zeros((8, LANES), f32) for _ in range(NBANDS + 1)]

    def step(g, totals):
        cells = field[pl.ds(pl.multiple_of(HALO + 16 * g, 16), 16), :]
        rows = pl.ds(pl.multiple_of(16 * g, 16), 16)
        new = []
        for i, total in enumerate(totals):
            v = cells * adjoint[i, rows, :]
            new.append(total + (v[0:8] + v[8:16]))
        return tuple(new)

    totals = lax.fori_loop(0, TR // 16, step, tuple(totals))
    row = lax.broadcasted_iota(jnp.int32, (8, LANES), 0)
    lane = lax.broadcasted_iota(jnp.int32, (8, LANES), 1)
    sums = normal[...]
    for i, total in enumerate(totals):
        sums = jnp.where((row == i) & (lane == NBANDS + 1), jnp.sum(total), sums)
    for k, out in enumerate(outs):
        start = pl.multiple_of(lax.rem(s + k, NY) * QROWS, QROWS)
        out[0:RQ, :] = field[pl.ds(start, RQ), :]
        out[RQ:, :] = sums


def merge_kernel(b0, b1, b2, b3, out):
    total = (b0[...] + b2[...]) + (b1[...] + b3[...])
    out[...] = jnp.broadcast_to(total[None], out.shape)


def lane_place(s, k):
    return pl.ds(pl.multiple_of(lax.rem(s + NY - k, NY) * LANES, LANES), LANES)


def split(v):
    high = v.astype(bf16)
    return high, (v - high.astype(f32)).astype(bf16)


def dot(a, b):
    return jnp.dot(a, b, preferred_element_type=f32)


def dot3(a, b):
    return dot(a[0], b[0]) + (dot(a[0], b[1]) + dot(a[1], b[0]))


def row_inside(info, rows):
    row = lax.broadcasted_iota(jnp.int32, (rows, 1), 0)
    return (row >= HALO * info[6]) & (row < rows - HALO * info[7])


def bands_kernel(info, pieces, row_h, row_l, col_h, col_l, turn, fields, coarse, raw):
    for k in range(NY):
        raw[:, :, LANES * k : LANES * (k + 1)] = pieces[k]
    inside = row_inside(info, RQ)
    for band in range(NBANDS + 1):
        cells = raw[band]
        fields[band] = dot(cells, turn[...]).astype(bf16)
        if band < NBANDS:
            down = split(dot(row_h[...], cells) + dot(row_l[...], cells))
            coarse[band] = jnp.where(inside, dot3(down, (col_h[...], col_l[...])), 0.0)


def write(slot, start, value):
    rows = slice(start, start + value.shape[0])
    lane = lax.broadcasted_iota(jnp.int32, (value.shape[0], LANES), 1)
    for t in range(NY):
        slot[t + 1, rows, :] = value[:, LANES * t : LANES * (t + 1)]
    before = pltpu.roll(value[:, 3 * LANES :], 1, 1)
    after = pltpu.roll(value[:, :LANES], LANES - 1, 1)
    slot[0, rows, :] = jnp.where(lane > 0, before, 0.0)
    slot[5, rows, :] = jnp.where(lane < LANES - 1, after, 0.0)


def put(slot, g, hidden):
    for t in range(6):
        part = slice(LANES * t, LANES * (t + 1))
        hidden[g, 0:128, part] = slot[t].astype(bf16)
        hidden[g + 1, 128:144, part] = slot[t, pl.ds(7, CH, stride=8), :].astype(bf16)
        hidden[g - 1, 144:160, part] = slot[t, pl.ds(0, CH, stride=8), :].astype(bf16)


def clear_ends(hidden):
    zero_rows = jnp.zeros((CH, 6 * LANES), bf16)
    hidden[1, 128:144, :] = zero_rows
    hidden[GROUPS - 2, 144:160, :] = zero_rows


def assemble_kernel(
    info, b0, b1, b2, b3, row_h, row_l, col_h, col_l, turn, fields_in, bands_in,
    coarse, hidden_out, natural, blended, group, fields, bands, hidden, in_sems, out_sems,
):
    s = info[3]
    arrays = ((fields_in, fields), (bands_in, bands))
    copies = [pltpu.make_async_copy(a, b, in_sems.at[i]) for i, (a, b) in enumerate(arrays)]
    for copy in copies:
        copy.start()
    for k, piece in enumerate((b0, b1, b2, b3)):
        natural[:, lane_place(s, k)] = piece[0:RQ, :]
    high, low = split(natural[...])
    down = split(dot3((row_h[...], row_l[...]), (high, low)))
    coarse[...] = jnp.where(
        row_inside(info, RQ), dot3(down, (col_h[...], col_l[...])), 0.0
    )
    blended[...] = dot(high, turn[...])
    clear_ends(hidden)
    for copy in copies:
        copy.wait()

    def leave(m):
        part = pl.ds(2 * m - 1, 2)
        return pltpu.make_async_copy(hidden.at[part], hidden_out.at[part], out_sems.at[m])

    def step(m, carry):
        rows = pl.ds(pl.multiple_of(16 * m, 16), 16)
        values = [jnp.zeros((16, COLS), f32), blended[rows, :], coarse[rows, :]]
        values.append(fields[NBANDS, rows, :].astype(f32))
        values += [fields[band, rows, :].astype(f32) for band in range(NBANDS)]
        values += [bands[band, rows, :] for band in range(NBANDS)]
        for half in range(2):
            g = 2 * m + half
            for channel, value in enumerate(values):
                write(group.at[half], 8 * channel, value[8 * half : 8 * half + 8])

            @pl.when((g >= 1) & (g <= GROUPS - 2))
            def _():
                put(group.at[half], g, hidden)

        @pl.when(m >= 1)
        def _():
            leave(m).start()

        return carry

    lax.fori_loop(0, GROUPS // 2, step, 0)
    for m in range(1, GROUPS // 2):
        leave(m).wait()


def assemble_scratch():
    return [
        pltpu.VMEM((RQ, COLS), f32),
        pltpu.VMEM((RQ, COLS), f32),
        pltpu.VMEM((2, 6, CH * 8, LANES), f32),
        pltpu.VMEM((NBANDS + 1, RQ, COLS), bf16),
        pltpu.VMEM((NBANDS, RQ, COLS), f32),
        pltpu.VMEM((GROUPS, KROWS, 6 * LANES), bf16),
        pltpu.SemaphoreType.DMA((2,)),
        pltpu.SemaphoreType.DMA((GROUPS // 2,)),
    ]


def solve(sums):
    row = lax.broadcasted_iota(jnp.int32, (8, LANES), 0)
    lane = lax.broadcasted_iota(jnp.int32, (8, LANES), 1)
    work = sums + jnp.where((row == lane) & (row <= NBANDS), ridge_term, 0.0)
    for pivot in range(NBANDS + 1):
        pivot_row = work[pivot : pivot + 1, :]
        pivot_value = jnp.sum(jnp.where(lane[0:1] == pivot, pivot_row, 0.0), axis=1, keepdims=True)
        scaled = pivot_row / pivot_value
        factor = jnp.sum(jnp.where(lane == pivot, work, 0.0), axis=1, keepdims=True)
        work = jnp.where(row == pivot, scaled, work - factor * scaled)
    picked = jnp.where(lane == NBANDS + 1, work, 0.0)
    return [jnp.sum(picked[i : i + 1, :]) for i in range(NBANDS + 1)]


def main_kernel(
    info, head, sums, coarse_in, fields_in, bands_in, kernels, biases, turn_back_in, stacked_in,
    o0, o1, o2, o3, fit_out, first_h, second_h, group, base, result,
    coarse, fields, bands, turn_back, stacked, sems, stack_sems,
):
    s = info[3]
    arrays = ((coarse_in, coarse), (fields_in, fields), (bands_in, bands))
    copies = [pltpu.make_async_copy(a, b, sems.at[i]) for i, (a, b) in enumerate(arrays)]
    for copy in copies:
        copy.start()
    steps = STEPS

    def stack_copy(i):
        part = pl.ds(1 + steps * i, steps)
        return pltpu.make_async_copy(stacked_in.at[part], stacked.at[part], stack_sems.at[i])

    for i in range((GROUPS - 2) // steps):
        stack_copy(i).start()
    turn_copy = pltpu.make_async_copy(turn_back_in, turn_back, sems.at[3])
    turn_copy.start()
    coefs = solve(jnp.sum(sums[...], axis=0))
    for i in range(NBANDS + 1):
        fit_out[i] = coefs[i]
    for copy in copies:
        copy.wait()
    clear_ends(first_h)
    clear_ends(second_h)

    def start(m, carry):
        rows = pl.ds(pl.multiple_of(16 * m, 16), 16)
        value = coarse[rows, :]
        for band in range(NBANDS):
            value = value + coefs[band + 1] * (
                fields[band, rows, :].astype(f32) - bands[band, rows, :]
            )
        lane = lax.broadcasted_iota(jnp.int32, (16, LANES), 1)
        base[rows, LANES : 5 * LANES] = value
        base[rows, 0:LANES] = jnp.where(lane > 0, pltpu.roll(value[:, 3 * LANES :], 1, 1), 0.0)
        base[rows, 5 * LANES :] = jnp.where(
            lane < LANES - 1, pltpu.roll(value[:, :LANES], LANES - 1, 1), 0.0
        )
        return carry

    lax.fori_loop(0, GROUPS // 2, start, 0, unroll=True)
    edge_row = lax.broadcasted_iota(jnp.int32, (CH, 6 * LANES), 0) == 0

    def with_base(g):
        own = stacked[g, 0:16, :].astype(f32)
        at = pl.multiple_of(8 * g, 8)
        own = jnp.concatenate([base[pl.ds(at, 8), :], own[8:16]], axis=0).astype(bf16)
        above = jnp.where(
            edge_row, base[pl.ds(8 * g - 1, 1), :], stacked[g, 128:144, :].astype(f32)
        )
        below = jnp.where(
            edge_row, base[pl.ds(8 * g + 8, 1), :], stacked[g, 144:160, :].astype(f32)
        )
        return jnp.concatenate(
            [own, stacked[g, 16:128, :], above.astype(bf16), below.astype(bf16)], axis=0
        )

    def convolved(layer, cells):
        spans = [slice(LANES * b, LANES * (b + 4)) for b in range(3)]
        taps = jnp.concatenate(
            [cells[0:128, span] for span in spans] + [cells[128:160, span] for span in spans],
            axis=0,
        )
        bias = jnp.concatenate([biases[layer]] * NY, axis=1)
        return jnp.maximum(dot(kernels[layer], taps) + bias, 0.0)

    for layer, following in enumerate((first_h, second_h)):

        def body(i, carry, layer=layer, following=following):
            if layer == 0:
                stack_copy(i).wait()
            for u in range(steps):
                g = 1 + steps * i + u
                cells = with_base(g) if layer == 0 else first_h[g]
                outside = ((g == 1) & (info[6] == 1)) | ((g == GROUPS - 2) & (info[7] == 1))
                keep = jnp.where(outside, 0.0, 1.0)
                write(group.at[u], 0, convolved(layer, cells) * keep)
                put(group.at[u], g, following)
            return carry

        lax.fori_loop(0, (GROUPS - 2) // steps, body, 0, unroll=True)

    def last(i, carry):
        mask = fields[NBANDS, pl.ds(pl.multiple_of(HALO + 32 * i, 32), 32), :].astype(f32)
        for u in range(4):
            g = 2 + 4 * i + u
            third = convolved(2, second_h[g]).astype(bf16).astype(f32)
            total = head[0] * third[0:8]
            for channel in range(1, CH):
                total = total + head[channel] * third[8 * channel : 8 * channel + 8]
            rows = pl.ds(pl.multiple_of(8 * g, 8), 8)
            out_rows = pl.ds(pl.multiple_of(8 * g - HALO, 8), 8)
            result[out_rows, :] = (
                base[rows, LANES : 5 * LANES] + mask[8 * u : 8 * u + 8] * total
            )
        return carry

    lax.fori_loop(0, QROWS // 32, last, 0, unroll=True)
    turn_copy.wait()
    high, low = split(result[...])
    result[...] = dot(high, turn_back[...]) + dot(low, turn_back[...])
    for k, out in enumerate((o0, o1, o2, o3)):
        out[...] = result[:, pl.ds(pl.multiple_of(lax.rem(s + k, NY) * LANES, LANES), LANES)]


def main_scratch():
    hidden = pltpu.VMEM((GROUPS, KROWS, 6 * LANES), bf16)
    return [
        hidden,
        hidden,
        pltpu.VMEM((STEPS, 6, CH * 8, LANES), f32),
        pltpu.VMEM((RQ, 6 * LANES), f32),
        pltpu.VMEM((QROWS, COLS), f32),
        pltpu.VMEM((RQ, COLS), f32),
        pltpu.VMEM((NBANDS + 1, RQ, COLS), bf16),
        pltpu.VMEM((NBANDS, RQ, COLS), f32),
        pltpu.VMEM((COLS, COLS), bf16),
        hidden,
        pltpu.SemaphoreType.DMA((4,)),
        pltpu.SemaphoreType.DMA(((GROUPS - 2) // STEPS,)),
    ]


def join_kernel(info, o0, o1, o2, o3, out):
    s = info[3]
    for k, piece in enumerate((o0, o1, o2, o3)):
        start = pl.multiple_of(lax.rem(s + NY - k, NY) * QROWS, QROWS)
        out[pl.ds(start, QROWS), :] = piece[...]


def band_matrix(rows, columns):
    offsets = np.arange(2 * RADIUS + 1) - RADIUS
    norm = np.sum(np.exp(-0.125 * offsets**2))
    apart = rows[:, None] - columns[None, :]
    weights = np.where(np.abs(apart) <= RADIUS, np.exp(-0.125 * apart**2) / norm, 0.0)
    high = weights.astype(bf16)
    return jnp.asarray(high), jnp.asarray((weights - high.astype(np.float64)).astype(bf16))


def matrices_kernel(taps, bias, kernels, biases):
    def iota(size, axis):
        return lax.broadcasted_iota(jnp.int32, (size, size), axis)

    tall = (CH * 8, CH)
    spread_rows = (
        lax.broadcasted_iota(jnp.int32, tall, 0) >> 3 == lax.broadcasted_iota(jnp.int32, tall, 1)
    )
    spread_rows = jnp.where(spread_rows, 1.0, 0.0).astype(bf16)
    wide = (CH, CH * 8)
    channel, lane = (lax.broadcasted_iota(jnp.int32, wide, a) for a in range(2))
    spread_lanes = jnp.where(lane >> 3 == channel, 1.0, 0.0).astype(bf16)
    r, l = iota(CH * 8, 0), iota(CH * 8, 1)
    up = (l & 7) - (r & 7)
    for layer in range(3):
        halo = jnp.zeros((CH * 8, CH * 8), f32)
        for b in range(3):
            own = jnp.zeros((CH * 8, CH * 8), f32)
            for a in range(3):
                column = dot(spread_rows, taps[layer, a, b]).astype(bf16)
                own = jnp.where(up == a - 1, dot(column, spread_lanes), own)
                if a == 1:
                    continue
                at = 32 * b + (0 if a == 0 else CH)
                placed = jnp.where(lane == channel + at, 1.0, 0.0).astype(bf16)
                halo = halo + jnp.where((r & 7) == (0 if a == 0 else 7), dot(column, placed), 0.0)
            kernels[layer, :, 128 * b : 128 * b + 128] = own.astype(bf16)
        kernels[layer, :, 384:480] = halo[:, 0:96].astype(bf16)
        for o in range(CH):
            biases[layer, 8 * o : 8 * o + 8, :] = jnp.broadcast_to(
                bias[CH * layer + o : CH * layer + o + 1, :], (8, LANES)
            )


def exchange(pieces, axis, route):
    return [pieces[0]] + [lax.ppermute(pieces[k], axis, route(k)) for k in range(1, 4)]


def shards(
    blk_temp, blk_qual, dest_tile, blk_offset, background, reflect, land,
    conv_first, bias_first, conv_second, bias_second, conv_third, bias_third, head,
):
    tile = lax.axis_index("tiles")
    s = lax.axis_index("swath")
    tiles = lax.axis_size("tiles")
    x, z, c = tile // (2 * NZ), (tile // 2) % NZ, tile % 2
    first = tile == 0
    last = tile == tiles - 1
    info = jnp.stack(
        [x, z, c, s, first, last, first & (s == 0), last & (s == NY - 1)]
    ).astype(jnp.int32)

    count = blk_temp.shape[0]
    down = [(i, i + 1) for i in range(tiles - 1)]
    up = [(i + 1, i) for i in range(tiles - 1)]

    def edge(last_rows):
        at = TR // HALO - 1 if last_rows else 0
        return [
            pl.BlockSpec((NBANDS, HALO, LANES), lambda i: (0, at, 0)),
            pl.BlockSpec((HALO, LANES), lambda i: (at, 0)),
            pl.BlockSpec((HALO, LANES), lambda i: (at, 0)),
        ]

    edges = [spec for pair in zip(edge(False), edge(True)) for spec in pair]
    row_h, row_l = band_matrix(np.arange(RQ), np.arange(RQ))
    natural = np.arange(COLS)
    place = NY * (natural % LANES) + natural // LANES
    col_h, col_l = band_matrix(natural, place)
    turn = jnp.asarray((natural[:, None] == place[None, :]).astype(bf16))
    turn_back = jnp.asarray((place[:, None] == natural[None, :]).astype(bf16))
    lanes = np.arange(2 * LANES)
    spot = np.where(lanes < LANES + HALO, lanes, lanes - LANES - 2 * HALO)
    spot = np.where(lanes < LANES + 2 * HALO, spot, 1000 * lanes)
    near_h, near_l = band_matrix(spot, spot)

    strip = sds((NBANDS + 1, STRIP, LANES), bf16)
    first_columns, last_columns = call(slab_kernel, (strip, strip), [VMEM] * 2, name="slab")(
        reflect, land
    )
    from_left = lax.ppermute(last_columns, "swath", [(i, i + 1) for i in range(NY - 1)])
    from_right = lax.ppermute(first_columns, "swath", [(i + 1, i) for i in range(NY - 1)])
    packed = call(
        pack_kernel,
        (sds((2 * count * BR + HALO, LANES), bf16),) * 4,
        [SMEM] * 3 + [VMEM] * 2,
        name="pack",
    )(info, dest_tile, blk_offset, blk_temp, blk_qual)
    block = sds(packed[0].shape, bf16)
    packed = tuple(packed[0:1]) + tuple(call(
        order_kernel, (block,) * 3, [ANY] * 5, place=ANY, alias={0: 0, 1: 1, 2: 2}, name="order"
    )(*packed[1:], from_left, from_right))
    edge_rows = sds((NBANDS + 3, HALO, 2 * LANES), bf16)
    top, bottom = call(
        edges_kernel, (edge_rows,) * 2, edges + [VMEM] * 2, grid=(1,), name="edges"
    )(reflect, reflect, land, land, background, background, from_left, from_right)
    above = lax.ppermute(bottom, "tiles", down)
    below = lax.ppermute(top, "tiles", up)

    adjoint, normal, window = call(
        adjoint_kernel,
        (
            sds((NBANDS + 1, TR, LANES), f32),
            sds((8, LANES), f32),
            sds((NBANDS + 1, WIN, LANES), bf16),
        ),
        [VMEM] * 10,
        scratch=[
            pltpu.VMEM((NBANDS + 1, WIN, LANES), bf16),
            pltpu.VMEM((NBANDS, RQ, 2 * LANES), f32),
        ],
        name="adjoint",
    )(reflect, land, above, below, from_left, from_right, row_h, row_l, near_h, near_l)
    taps = jnp.transpose(jnp.stack([conv_first, conv_second, conv_third]), (0, 3, 4, 1, 2))
    bias = jnp.concatenate([bias_first, bias_second, bias_third])
    kernels, biases = call(
        matrices_kernel,
        (sds((3, CH * 8, 3 * KROWS), bf16), sds((3, CH * 8, LANES), f32)),
        [VMEM] * 2,
        name="matrices",
    )(taps, jnp.broadcast_to(bias[:, None], (3 * CH, LANES)))
    weights = head.astype(f32)

    chip = exchange(packed, "swath", along_y)
    chip[1] = call(
        order_kernel, (block,), [ANY] * 3, place=ANY, alias={0: 0}, name="order"
    )(chip[1], adjoint, kernels)[0]
    cut = call(
        cut_kernel,
        sds((NY, NBANDS + 1, RQ, LANES), bf16),
        [VMEM] + [ANY],
        name="cut",
    )(window, chip[2])
    pieces = lax.all_to_all(cut, "swath", split_axis=0, concat_axis=0, tiled=True)
    fields, bands = call(
        bands_kernel,
        (sds((NBANDS + 1, RQ, COLS), bf16), sds((NBANDS, RQ, COLS), f32)),
        [SMEM] + [VMEM] * 6,
        scratch=[pltpu.VMEM((NBANDS + 1, RQ, COLS), bf16)],
        flops=2 * 6 * 160 * 512 * (320 + 1536),
        nbytes=10 << 20,
        name="bands",
    )(info, pieces, row_h, row_l, col_h, col_l, turn)
    chip[2] = call(
        order_kernel, (block,), [ANY] * 2, place=ANY, alias={0: 0}, name="order"
    )(chip[2], cut)[0]
    chip = chip + [lax.ppermute(p, "tiles", core_pair) for p in chip]

    part = sds((4, WIN, LANES), bf16)
    routed = call(
        scatter_kernel,
        (part,) * 8,
        [SMEM] + [ANY] * 9,
        scratch=scatter_scratch(2 * count * BR),
        place=ANY,
        flops=96 * 128 * 128 * 8,
        nbytes=12 << 20,
        name="scatter",
    )(info, *chip, cut)
    nums = exchange(routed[0:4], "tiles", along_x)
    dens = exchange(routed[4:8], "tiles", along_z)

    one = sds((WIN, LANES), f32)
    summed = call(sum_kernel, (one,) * 4, [VMEM] * 4 + [ANY], nbytes=3 << 20, name="add")
    nums = summed(*nums, fields)
    dens = summed(*dens, fields)
    nums = exchange(nums, "tiles", along_z)
    dens = exchange(dens, "tiles", along_x)
    rows = call(
        blend_kernel,
        (sds((RQ + 8, LANES), f32),) * 4,
        [SMEM] + [VMEM] * 13,
        scratch=[pltpu.VMEM((WIN, LANES), f32)],
        nbytes=3 << 20,
        name="blend",
    )(info, *nums, *dens, background, above, below, adjoint, normal)
    rows = exchange(rows, "swath", along_y)
    sums = call(
        merge_kernel,
        sds((tiles, 8, LANES), f32),
        [pl.BlockSpec((8, LANES), lambda i: (RQ // 8, 0))] * 4,
        grid=(1,),
        name="merge",
    )(*rows)
    sums = lax.all_to_all(sums, "tiles", split_axis=0, concat_axis=0, tiled=True)
    coarse, stacked = call(
        assemble_kernel,
        (sds((RQ, COLS), f32), sds((GROUPS, KROWS, 6 * LANES), bf16)),
        [SMEM] + [VMEM] * 9 + [ANY] * 2,
        scratch=assemble_scratch(),
        place=(VMEM, ANY),
        flops=2 * 160 * 512 * (480 + 1536),
        nbytes=8 << 20,
        name="assemble",
    )(info, *rows, row_h, row_l, col_h, col_l, turn, fields, bands)
    *sharp, fit_coefs = call(
        main_kernel,
        (sds((QROWS, LANES), f32),) * 4 + (sds((NBANDS + 1,), f32),),
        [SMEM, SMEM, VMEM] + [ANY] * 3 + [VMEM] * 2 + [ANY] * 2,
        scratch=main_scratch(),
        flops=3 * 18 * 2 * 384 * 160 * 512,
        nbytes=8 << 20,
        name="convolve",
    )(info, weights, sums, coarse, fields, bands, kernels, biases, turn_back, stacked)
    sharp = exchange(sharp, "swath", along_y)
    out = call(join_kernel, sds((TR, LANES), f32), [SMEM] + [VMEM] * 4, name="join")(info, *sharp)
    return out, fit_coefs


def solution(mesh):
    placed = (
        P(("tiles", "swath"), None, None),
        P(("tiles", "swath"), None, None),
        P(("tiles", "swath")),
        P(("tiles", "swath")),
        P("tiles", "swath"),
        P(None, "tiles", "swath"),
        P("tiles", "swath"),
        P(),
        P(),
        P(),
        P(),
        P(),
        P(),
        P(),
    )
    return jax.shard_map(
        shards, mesh=mesh, in_specs=placed, out_specs=(P("tiles", "swath"), P()), check_vma=False
    )
```

```python
import jax
import jax.numpy as jnp
import numpy as np
from jax import lax
from jax.experimental import pallas as pl
from jax.experimental.pallas import tpu as pltpu
from jax.sharding import PartitionSpec as P

TR = 512
BR = 128
RADIUS = 7
NBANDS = 6
CH = 16
NX = 4
NZ = 4
NY = 4
LANES = 128
HALO = 16
WIN = TR + 2 * HALO
ACC = WIN + 2 * HALO
QROWS = TR // NY
RQ = QROWS + 2 * HALO
COLS = NY * LANES
GROUPS = RQ // 8
KROWS = CH * 8 + 2 * CH
STRIP = 64
STEPS = 6
STRIPS = TR // STRIP

prior_weight = 0.5
ridge_term = 1.0
f32 = jnp.float32
bf16 = jnp.bfloat16
VMEM = pl.BlockSpec(memory_space=pltpu.VMEM)
SMEM = pl.BlockSpec(memory_space=pltpu.SMEM)
ANY = pl.BlockSpec(memory_space=pl.ANY)


def tile_id(x, z, c):
    return (x * NZ + z) * 2 + c


def along_y(k):
    return [(i, (i + k) % NY) for i in range(NY)]


def along_x(k):
    return [
        (tile_id(x, z, c), tile_id((x + k) % NX, z, c))
        for x in range(NX)
        for z in range(NZ)
        for c in range(2)
    ]


def along_z(k):
    return [
        (tile_id(x, z, c), tile_id(x, (z + k) % NZ, c))
        for x in range(NX)
        for z in range(NZ)
        for c in range(2)
    ]


core_pair = [(i, i ^ 1) for i in range(2 * NX * NZ)]


def call(kernel, outs, ins, scratch=(), flops=0, nbytes=0, name=None, grid=(), place=VMEM, alias={}):
    return pl.pallas_call(
        kernel,
        grid=grid,
        out_shape=outs,
        in_specs=ins,
        out_specs=place
        if isinstance(place, tuple)
        else jax.tree.map(lambda o: SMEM if o.shape == (NBANDS + 1,) else place, outs),
        scratch_shapes=list(scratch),
        input_output_aliases=alias,
        compiler_params=pltpu.CompilerParams(vmem_limit_bytes=56 * 1024 * 1024),
        cost_estimate=pl.CostEstimate(flops=flops, bytes_accessed=nbytes, transcendentals=0),
        name=name,
    )


def sds(shape, dtype):
    return jax.ShapeDtypeStruct(shape, dtype)


def add_blocks(meta, info, count, arrivals, add):
    c = info[2]
    for piece in range(8):
        arrivals[piece].wait()

        def body(j, carry, piece=piece):
            code = meta[piece, j]
            tile = code >> 9
            off = code & (TR - 1)
            mine = (tile & 1) == c

            @pl.when(mine)
            def _():
                add(piece, j, tile >> 1, off + 2 * HALO, 0, BR)

            @pl.when(jnp.logical_not(mine) & ((off > TR - BR - HALO) | (off < HALO)))
            def _():
                @pl.when((off > TR - BR - HALO) & (tile < 2 * NX * NZ - 1))
                def _():
                    add(piece, j, (tile + 1) >> 1, off - (TR - BR - HALO), BR - HALO, HALO)

                @pl.when((off < HALO) & (tile > 0))
                def _():
                    add(piece, j, (tile - 1) >> 1, off + 2 * HALO + TR, 0, HALO)

            return carry

        lax.fori_loop(0, count, body, 0, unroll=4)


def pack_kernel(info, dest, offset, temp, qual, *outs):
    s = info[3]
    count = temp.shape[0]
    lane = lax.broadcasted_iota(jnp.int32, (HALO, LANES), 1)
    row = lax.broadcasted_iota(jnp.int32, (HALO, LANES), 0)
    places = jnp.zeros((HALO, LANES), jnp.int32)
    for j in range(count):
        numbers = (dest[j], offset[j] >> 4, offset[j] & 15)
        for i, number in enumerate(numbers):
            places = jnp.where((lane == j) & (row == i), number, places)
    places = places.astype(f32).astype(bf16)
    for k, out in enumerate(outs):
        lanes = pl.ds(pl.multiple_of(lax.rem(s + k, NY) * LANES, LANES), LANES)
        for j in range(count):
            out[BR * j : BR * (j + 1), :] = qual[j, :, lanes]
            out[BR * (count + j) : BR * (count + j + 1), :] = temp[j, :, lanes]
        out[2 * count * BR :, :] = places

def scatter_kernel(info, *refs):
    pieces, outs = refs[0:8], refs[9:17]
    acc_n, acc_d, places, meta, sem, held, numbers, staged, in_sems, place_sems, out_sems = refs[17:]
    x, z = info[0], info[1]
    count = (pieces[0].shape[0] - HALO) // (2 * BR)
    small, large = [], []
    for i, piece in enumerate(pieces):
        tail = piece.at[pl.ds(2 * count * BR, HALO)]
        small.append(pltpu.make_async_copy(tail, numbers.at[i], place_sems.at[i]))
        small[i].start()
    for i, piece in enumerate(pieces):
        body = piece.at[pl.ds(0, 2 * count * BR)]
        large.append(pltpu.make_async_copy(body, held.at[i], in_sems.at[i]))
        large[i].start()
    for i in range(8):
        small[i].wait()
        number = numbers[i].astype(f32)
        code = number[0:1] * TR + number[1:2] * 16.0 + number[2:3]
        places[i : i + 1, :] = code.astype(jnp.int32)
    copy = pltpu.make_async_copy(places, meta, sem)
    copy.start()

    def clear(i, carry):
        acc_n[i] = jnp.zeros((ACC, LANES), f32)
        acc_d[i] = jnp.zeros((ACC, LANES), f32)
        return carry

    def add(piece, j, slot, start, row, rows):
        span = pl.ds(start, rows)
        at = pl.multiple_of(j * BR + row, HALO)
        q = held[piece, pl.ds(at, rows), :].astype(f32)
        t = held[piece, pl.ds(count * BR + at, rows), :].astype(f32)
        acc_d[slot, span, :] = acc_d[slot, span, :] + q
        acc_n[slot, span, :] = acc_n[slot, span, :] + q * t

    lax.fori_loop(0, NX * NZ, clear, 0)
    copy.wait()
    add_blocks(meta, info, count, large, add)
    leaving = []
    for kx in range(NX):
        for kz in range(NZ):
            slot = lax.rem(x + kx, NX) * NZ + lax.rem(z + kz, NZ)
            targets = (outs[kx].at[kz], outs[NX + kz].at[kx])
            for acc, target in zip((acc_n, acc_d), targets):
                i = len(leaving)
                staged[i] = acc[slot, HALO : HALO + WIN, :].astype(bf16)
                leaving.append(pltpu.make_async_copy(staged.at[i], target, out_sems.at[i]))
                leaving[i].start()
    for copy in leaving:
        copy.wait()


def scatter_scratch(rows):
    return [pltpu.VMEM((NX * NZ, ACC, LANES), f32)] * 2 + [
        pltpu.VMEM((8, LANES), jnp.int32),
        pltpu.SMEM((8, LANES), jnp.int32),
        pltpu.SemaphoreType.DMA,
        pltpu.VMEM((8, rows, LANES), bf16),
        pltpu.VMEM((8, HALO, LANES), bf16),
        pltpu.VMEM((2 * NX * NZ, WIN, LANES), bf16),
        pltpu.SemaphoreType.DMA((8,)),
        pltpu.SemaphoreType.DMA((8,)),
        pltpu.SemaphoreType.DMA((2 * NX * NZ,)),
    ]


def sum_kernel(a, b, c, d, *refs):
    for k, out in enumerate(refs[-4:]):
        out[...] = (a[k].astype(f32) + b[k].astype(f32)) + (c[k].astype(f32) + d[k].astype(f32))


def order_kernel(*refs):
    pass


def slab_kernel(reflect, land, first, last):
    lane = lax.broadcasted_iota(jnp.int32, (STRIP, LANES), 1)

    for plane in range(NBANDS + 1):
        sides = [jnp.zeros((STRIP, LANES), f32) for _ in range(2)]
        for i in range(STRIPS):
            rows = slice(STRIP * i, STRIP * (i + 1))
            cells = (reflect[plane, rows, :] if plane < NBANDS else land[rows, :]).astype(f32)
            for side, source in enumerate((0, LANES - HALO)):
                moved = pltpu.roll(cells, (HALO * i - source) % LANES, 1)
                sides[side] = jnp.where(lane >> 4 == i, moved, sides[side])
        first[plane] = sides[0].astype(bf16)
        last[plane] = sides[1].astype(bf16)


def beside_of(left, right, i):
    lane = lax.broadcasted_iota(jnp.int32, left.shape, 1)
    after = pltpu.roll(right, (-HALO * i) % LANES, 1)
    before = pltpu.roll(left, (HALO - HALO * i) % LANES, 1)
    return jnp.where(lane < HALO, after, jnp.where(lane < 2 * HALO, before, 0.0)).astype(bf16)


def edges_kernel(r0, r1, l0, l1, b0, b1, left, right, top, bottom):
    own = slice(0, LANES)
    sides = ((top, r0, l0, b0, 0, 0), (bottom, r1, l1, b1, STRIPS - 1, STRIP - HALO))
    for out, reflect, land, background, strip, row in sides:
        out[0:NBANDS, :, own] = reflect[...]
        out[NBANDS, :, own] = land[...].astype(f32).astype(bf16)
        high, low = split(background[...])
        out[NBANDS + 1, :, own] = high
        out[NBANDS + 2, :, own] = low
        for plane in range(NBANDS + 1):
            rows = slice(row, row + HALO)
            out[plane, :, LANES:] = beside_of(
                left[plane, rows, :].astype(f32), right[plane, rows, :].astype(f32), strip
            )
        for plane in range(NBANDS + 1, NBANDS + 3):
            out[plane, :, LANES:] = jnp.zeros((HALO, LANES), bf16)


def adjoint_kernel(
    reflect, land, above, below, left, right, row_h, row_l, col_h, col_l,
    adjoint, normal, window, beside, bands,
):
    for rows, edge in ((slice(0, HALO), above), (slice(HALO + TR, WIN), below)):
        window[:, rows, :] = edge[0 : NBANDS + 1, :, 0:LANES]
        beside[:, rows, :] = edge[0 : NBANDS + 1, :, LANES:]
    window[0:NBANDS, HALO : HALO + TR, :] = reflect[...]
    window[NBANDS, HALO : HALO + TR, :] = land[...].astype(f32).astype(bf16)

    def spread(plane, carry):
        before = left[plane].astype(f32)
        after = right[plane].astype(f32)
        for i in range(STRIPS):
            rows = slice(HALO + STRIP * i, HALO + STRIP * (i + 1))
            beside[plane, rows, :] = beside_of(before, after, i)
        return carry

    lax.fori_loop(0, NBANDS + 1, spread, 0)
    pairs = [(i, j) for i in range(NBANDS + 1) for j in range(i, NBANDS + 1)]
    own = slice(HALO, HALO + QROWS)

    def quarter(q, sums):
        rows = pl.ds(pl.multiple_of(QROWS * q, QROWS), RQ)

        def cells(plane):
            return jnp.concatenate([window[plane, rows, :], beside[plane, rows, :]], axis=1)

        land = cells(NBANDS).astype(f32)
        for band in range(NBANDS):
            x = cells(band)
            down = split(dot(row_h[...], x) + dot(row_l[...], x))
            bands[band] = dot3(down, (col_h[...], col_l[...]))
        for i in range(NBANDS + 1):
            value = split(land if i == 0 else land * bands[i - 1])
            down = split(dot3((row_h[own, :], row_l[own, :]), value))
            adjoint[i, pl.ds(pl.multiple_of(QROWS * q, QROWS), QROWS), :] = dot3(
                down, (col_h[:, 0:LANES], col_l[:, 0:LANES])
            )

        def step(g, sums):
            at = pl.multiple_of(HALO + 16 * g, 16)
            part = pl.ds(at, 16)
            mask = window[NBANDS, pl.ds(pl.multiple_of(QROWS * q + at, 16), 16), :].astype(f32)
            x = [None] + [bands[band, part, 0:LANES] for band in range(NBANDS)]
            mx = [mask] + [mask * x[i] for i in range(1, NBANDS + 1)]
            new = []
            for (i, j), total in zip(pairs, sums):
                v = mx[j] if i == 0 else mx[i] * x[j]
                new.append(total + (v[0:8] + v[8:16]))
            return tuple(new)

        return lax.fori_loop(0, QROWS // 16, step, sums)

    sums = lax.fori_loop(0, NY, quarter, tuple(jnp.zeros((8, LANES), f32) for _ in pairs))
    row = lax.broadcasted_iota(jnp.int32, (8, LANES), 0)
    lane = lax.broadcasted_iota(jnp.int32, (8, LANES), 1)
    result = jnp.zeros((8, LANES), f32)
    for (i, j), total in zip(pairs, sums):
        here = ((row == i) & (lane == j)) | ((row == j) & (lane == i))
        result = jnp.where(here, jnp.sum(total), result)
    normal[...] = result


def cut_kernel(window, after, out):
    for k in range(NY):
        out[k] = window[:, QROWS * k : QROWS * k + RQ, :]


def blend_kernel(info, *refs):
    nums, dens = refs[0:4], refs[4:8]
    background, above, below = refs[8:11]
    adjoint, normal = refs[11], refs[12]
    outs, field = refs[13:17], refs[17]
    first, last, s = info[4], info[5], info[3]
    num = nums[0][...].astype(f32)
    den = dens[0][...].astype(f32)
    for n in nums[1:]:
        num = num + n[...].astype(f32)
    for d in dens[1:]:
        den = den + d[...].astype(f32)
    ends = [
        edge[NBANDS + 1, :, 0:LANES].astype(f32) + edge[NBANDS + 2, :, 0:LANES].astype(f32) for edge in (above, below)
    ]
    prior = jnp.concatenate([ends[0], background[...], ends[1]], axis=0)
    row = lax.broadcasted_iota(jnp.int32, (WIN, LANES), 0)
    inside = (row >= HALO * first) & (row < WIN - HALO * last)
    blended = (prior_weight * prior + num) / (prior_weight + den)
    field[...] = jnp.where(inside, blended, 0.0)
    totals = [jnp.zeros((8, LANES), f32) for _ in range(NBANDS + 1)]

    def step(g, totals):
        cells = field[pl.ds(pl.multiple_of(HALO + 16 * g, 16), 16), :]
        rows = pl.ds(pl.multiple_of(16 * g, 16), 16)
        new = []
        for i, total in enumerate(totals):
            v = cells * adjoint[i, rows, :]
            new.append(total + (v[0:8] + v[8:16]))
        return tuple(new)

    totals = lax.fori_loop(0, TR // 16, step, tuple(totals), unroll=4)
    row = lax.broadcasted_iota(jnp.int32, (8, LANES), 0)
    lane = lax.broadcasted_iota(jnp.int32, (8, LANES), 1)
    sums = normal[...]
    for i, total in enumerate(totals):
        sums = jnp.where((row == i) & (lane == NBANDS + 1), jnp.sum(total), sums)
    for k, out in enumerate(outs):
        start = pl.multiple_of(lax.rem(s + k, NY) * QROWS, QROWS)
        out[0:RQ, :] = field[pl.ds(start, RQ), :]
        out[RQ:, :] = sums


def merge_kernel(b0, b1, b2, b3, out):
    total = (b0[...] + b2[...]) + (b1[...] + b3[...])
    out[...] = jnp.broadcast_to(total[None], out.shape)


def lane_place(s, k):
    return pl.ds(pl.multiple_of(lax.rem(s + NY - k, NY) * LANES, LANES), LANES)


def split(v):
    high = v.astype(bf16)
    return high, (v - high.astype(f32)).astype(bf16)


def dot(a, b):
    return jnp.dot(a, b, preferred_element_type=f32)


def dot3(a, b):
    return dot(a[0], b[0]) + (dot(a[0], b[1]) + dot(a[1], b[0]))


def row_inside(info, rows):
    row = lax.broadcasted_iota(jnp.int32, (rows, 1), 0)
    return (row >= HALO * info[6]) & (row < rows - HALO * info[7])


def bands_kernel(info, pieces, row_h, row_l, col_h, col_l, turn, fields, coarse, raw):
    for k in range(NY):
        raw[:, :, LANES * k : LANES * (k + 1)] = pieces[k]
    inside = row_inside(info, RQ)
    for band in range(NBANDS + 1):
        cells = raw[band]
        fields[band] = dot(cells, turn[...]).astype(bf16)
        if band < NBANDS:
            down = split(dot(row_h[...], cells) + dot(row_l[...], cells))
            coarse[band] = jnp.where(inside, dot3(down, (col_h[...], col_l[...])), 0.0)


def write(slot, start, value):
    rows = slice(start, start + value.shape[0])
    lane = lax.broadcasted_iota(jnp.int32, (value.shape[0], LANES), 1)
    for t in range(NY):
        slot[t + 1, rows, :] = value[:, LANES * t : LANES * (t + 1)]
    before = pltpu.roll(value[:, 3 * LANES :], 1, 1)
    after = pltpu.roll(value[:, :LANES], LANES - 1, 1)
    slot[0, rows, :] = jnp.where(lane > 0, before, 0.0)
    slot[5, rows, :] = jnp.where(lane < LANES - 1, after, 0.0)


def put(slot, g, hidden):
    for t in range(6):
        part = slice(LANES * t, LANES * (t + 1))
        hidden[g, 0:128, part] = slot[t].astype(bf16)
        hidden[g + 1, 128:144, part] = slot[t, pl.ds(7, CH, stride=8), :].astype(bf16)
        hidden[g - 1, 144:160, part] = slot[t, pl.ds(0, CH, stride=8), :].astype(bf16)


def clear_ends(hidden):
    zero_rows = jnp.zeros((CH, 6 * LANES), bf16)
    hidden[1, 128:144, :] = zero_rows
    hidden[GROUPS - 2, 144:160, :] = zero_rows


def assemble_kernel(
    info, b0, b1, b2, b3, row_h, row_l, col_h, col_l, turn, fields_in, bands_in,
    coarse, hidden_out, natural, blended, group, fields, bands, hidden, in_sems, out_sems,
):
    s = info[3]
    arrays = ((fields_in, fields), (bands_in, bands))
    copies = [pltpu.make_async_copy(a, b, in_sems.at[i]) for i, (a, b) in enumerate(arrays)]
    for copy in copies:
        copy.start()
    for k, piece in enumerate((b0, b1, b2, b3)):
        natural[:, lane_place(s, k)] = piece[0:RQ, :]
    high, low = split(natural[...])
    down = split(dot3((row_h[...], row_l[...]), (high, low)))
    coarse[...] = jnp.where(
        row_inside(info, RQ), dot3(down, (col_h[...], col_l[...])), 0.0
    )
    blended[...] = dot(high, turn[...])
    clear_ends(hidden)
    for copy in copies:
        copy.wait()

    def leave(m):
        part = pl.ds(2 * m - 1, 2)
        return pltpu.make_async_copy(hidden.at[part], hidden_out.at[part], out_sems.at[m])

    def step(m, carry):
        rows = pl.ds(pl.multiple_of(16 * m, 16), 16)
        values = [jnp.zeros((16, COLS), f32), blended[rows, :], coarse[rows, :]]
        values.append(fields[NBANDS, rows, :].astype(f32))
        values += [fields[band, rows, :].astype(f32) for band in range(NBANDS)]
        values += [bands[band, rows, :] for band in range(NBANDS)]
        for half in range(2):
            g = 2 * m + half
            for channel, value in enumerate(values):
                write(group.at[half], 8 * channel, value[8 * half : 8 * half + 8])

            @pl.when((g >= 1) & (g <= GROUPS - 2))
            def _():
                put(group.at[half], g, hidden)

        @pl.when(m >= 1)
        def _():
            leave(m).start()

        return carry

    lax.fori_loop(0, GROUPS // 2, step, 0)
    for m in range(1, GROUPS // 2):
        leave(m).wait()


def assemble_scratch():
    return [
        pltpu.VMEM((RQ, COLS), f32),
        pltpu.VMEM((RQ, COLS), f32),
        pltpu.VMEM((2, 6, CH * 8, LANES), f32),
        pltpu.VMEM((NBANDS + 1, RQ, COLS), bf16),
        pltpu.VMEM((NBANDS, RQ, COLS), f32),
        pltpu.VMEM((GROUPS, KROWS, 6 * LANES), bf16),
        pltpu.SemaphoreType.DMA((2,)),
        pltpu.SemaphoreType.DMA((GROUPS // 2,)),
    ]


def solve(sums):
    row = lax.broadcasted_iota(jnp.int32, (8, LANES), 0)
    lane = lax.broadcasted_iota(jnp.int32, (8, LANES), 1)
    work = sums + jnp.where((row == lane) & (row <= NBANDS), ridge_term, 0.0)
    for pivot in range(NBANDS + 1):
        pivot_row = work[pivot : pivot + 1, :]
        pivot_value = jnp.sum(jnp.where(lane[0:1] == pivot, pivot_row, 0.0), axis=1, keepdims=True)
        scaled = pivot_row / pivot_value
        factor = jnp.sum(jnp.where(lane == pivot, work, 0.0), axis=1, keepdims=True)
        work = jnp.where(row == pivot, scaled, work - factor * scaled)
    picked = jnp.where(lane == NBANDS + 1, work, 0.0)
    return [jnp.sum(picked[i : i + 1, :]) for i in range(NBANDS + 1)]


def main_kernel(
    info, head, sums, coarse_in, fields_in, bands_in, kernels, biases, turn_back_in, stacked_in,
    o0, o1, o2, o3, fit_out, first_h, second_h, group, base, result,
    coarse, fields, bands, turn_back, stacked, sems, stack_sems,
):
    s = info[3]
    arrays = ((coarse_in, coarse), (fields_in, fields), (bands_in, bands))
    copies = [pltpu.make_async_copy(a, b, sems.at[i]) for i, (a, b) in enumerate(arrays)]
    for copy in copies:
        copy.start()
    steps = STEPS

    def stack_copy(i):
        part = pl.ds(1 + steps * i, steps)
        return pltpu.make_async_copy(stacked_in.at[part], stacked.at[part], stack_sems.at[i])

    for i in range((GROUPS - 2) // steps):
        stack_copy(i).start()
    turn_copy = pltpu.make_async_copy(turn_back_in, turn_back, sems.at[3])
    turn_copy.start()
    coefs = solve(jnp.sum(sums[...], axis=0))
    for i in range(NBANDS + 1):
        fit_out[i] = coefs[i]
    for copy in copies:
        copy.wait()
    clear_ends(first_h)
    clear_ends(second_h)

    def start(m, carry):
        rows = pl.ds(pl.multiple_of(16 * m, 16), 16)
        value = coarse[rows, :]
        for band in range(NBANDS):
            value = value + coefs[band + 1] * (
                fields[band, rows, :].astype(f32) - bands[band, rows, :]
            )
        lane = lax.broadcasted_iota(jnp.int32, (16, LANES), 1)
        base[rows, LANES : 5 * LANES] = value
        base[rows, 0:LANES] = jnp.where(lane > 0, pltpu.roll(value[:, 3 * LANES :], 1, 1), 0.0)
        base[rows, 5 * LANES :] = jnp.where(
            lane < LANES - 1, pltpu.roll(value[:, :LANES], LANES - 1, 1), 0.0
        )
        return carry

    lax.fori_loop(0, GROUPS // 2, start, 0, unroll=True)
    edge_row = lax.broadcasted_iota(jnp.int32, (CH, 6 * LANES), 0) == 0

    def with_base(g):
        own = stacked[g, 0:16, :].astype(f32)
        at = pl.multiple_of(8 * g, 8)
        own = jnp.concatenate([base[pl.ds(at, 8), :], own[8:16]], axis=0).astype(bf16)
        above = jnp.where(
            edge_row, base[pl.ds(8 * g - 1, 1), :], stacked[g, 128:144, :].astype(f32)
        )
        below = jnp.where(
            edge_row, base[pl.ds(8 * g + 8, 1), :], stacked[g, 144:160, :].astype(f32)
        )
        return jnp.concatenate(
            [own, stacked[g, 16:128, :], above.astype(bf16), below.astype(bf16)], axis=0
        )

    def convolved(layer, cells):
        spans = [slice(LANES * b, LANES * (b + 4)) for b in range(3)]
        taps = jnp.concatenate(
            [cells[0:128, span] for span in spans] + [cells[128:160, span] for span in spans],
            axis=0,
        )
        bias = jnp.concatenate([biases[layer]] * NY, axis=1)
        return jnp.maximum(dot(kernels[layer], taps) + bias, 0.0)

    for layer, following in enumerate((first_h, second_h)):

        def body(i, carry, layer=layer, following=following):
            if layer == 0:
                stack_copy(i).wait()
            for u in range(steps):
                g = 1 + steps * i + u
                cells = with_base(g) if layer == 0 else first_h[g]
                outside = ((g == 1) & (info[6] == 1)) | ((g == GROUPS - 2) & (info[7] == 1))
                keep = jnp.where(outside, 0.0, 1.0)
                write(group.at[u], 0, convolved(layer, cells) * keep)
                put(group.at[u], g, following)
            return carry

        lax.fori_loop(0, (GROUPS - 2) // steps, body, 0, unroll=True)

    def last(i, carry):
        mask = fields[NBANDS, pl.ds(pl.multiple_of(HALO + 32 * i, 32), 32), :].astype(f32)
        for u in range(4):
            g = 2 + 4 * i + u
            third = convolved(2, second_h[g]).astype(bf16).astype(f32)
            total = head[0] * third[0:8]
            for channel in range(1, CH):
                total = total + head[channel] * third[8 * channel : 8 * channel + 8]
            rows = pl.ds(pl.multiple_of(8 * g, 8), 8)
            out_rows = pl.ds(pl.multiple_of(8 * g - HALO, 8), 8)
            result[out_rows, :] = (
                base[rows, LANES : 5 * LANES] + mask[8 * u : 8 * u + 8] * total
            )
        return carry

    lax.fori_loop(0, QROWS // 32, last, 0, unroll=True)
    turn_copy.wait()
    high, low = split(result[...])
    result[...] = dot(high, turn_back[...]) + dot(low, turn_back[...])
    for k, out in enumerate((o0, o1, o2, o3)):
        out[...] = result[:, pl.ds(pl.multiple_of(lax.rem(s + k, NY) * LANES, LANES), LANES)]


def main_scratch():
    hidden = pltpu.VMEM((GROUPS, KROWS, 6 * LANES), bf16)
    return [
        hidden,
        hidden,
        pltpu.VMEM((STEPS, 6, CH * 8, LANES), f32),
        pltpu.VMEM((RQ, 6 * LANES), f32),
        pltpu.VMEM((QROWS, COLS), f32),
        pltpu.VMEM((RQ, COLS), f32),
        pltpu.VMEM((NBANDS + 1, RQ, COLS), bf16),
        pltpu.VMEM((NBANDS, RQ, COLS), f32),
        pltpu.VMEM((COLS, COLS), bf16),
        hidden,
        pltpu.SemaphoreType.DMA((4,)),
        pltpu.SemaphoreType.DMA(((GROUPS - 2) // STEPS,)),
    ]


def join_kernel(info, o0, o1, o2, o3, out):
    s = info[3]
    for k, piece in enumerate((o0, o1, o2, o3)):
        start = pl.multiple_of(lax.rem(s + NY - k, NY) * QROWS, QROWS)
        out[pl.ds(start, QROWS), :] = piece[...]


def band_matrix(rows, columns):
    offsets = np.arange(2 * RADIUS + 1) - RADIUS
    norm = np.sum(np.exp(-0.125 * offsets**2))
    apart = rows[:, None] - columns[None, :]
    weights = np.where(np.abs(apart) <= RADIUS, np.exp(-0.125 * apart**2) / norm, 0.0)
    high = weights.astype(bf16)
    return jnp.asarray(high), jnp.asarray((weights - high.astype(np.float64)).astype(bf16))


def matrices_kernel(taps, bias, kernels, biases):
    def iota(size, axis):
        return lax.broadcasted_iota(jnp.int32, (size, size), axis)

    tall = (CH * 8, CH)
    spread_rows = (
        lax.broadcasted_iota(jnp.int32, tall, 0) >> 3 == lax.broadcasted_iota(jnp.int32, tall, 1)
    )
    spread_rows = jnp.where(spread_rows, 1.0, 0.0).astype(bf16)
    wide = (CH, CH * 8)
    channel, lane = (lax.broadcasted_iota(jnp.int32, wide, a) for a in range(2))
    spread_lanes = jnp.where(lane >> 3 == channel, 1.0, 0.0).astype(bf16)
    r, l = iota(CH * 8, 0), iota(CH * 8, 1)
    up = (l & 7) - (r & 7)
    for layer in range(3):
        halo = jnp.zeros((CH * 8, CH * 8), f32)
        for b in range(3):
            own = jnp.zeros((CH * 8, CH * 8), f32)
            for a in range(3):
                column = dot(spread_rows, taps[layer, a, b]).astype(bf16)
                own = jnp.where(up == a - 1, dot(column, spread_lanes), own)
                if a == 1:
                    continue
                at = 32 * b + (0 if a == 0 else CH)
                placed = jnp.where(lane == channel + at, 1.0, 0.0).astype(bf16)
                halo = halo + jnp.where((r & 7) == (0 if a == 0 else 7), dot(column, placed), 0.0)
            kernels[layer, :, 128 * b : 128 * b + 128] = own.astype(bf16)
        kernels[layer, :, 384:480] = halo[:, 0:96].astype(bf16)
        for o in range(CH):
            biases[layer, 8 * o : 8 * o + 8, :] = jnp.broadcast_to(
                bias[CH * layer + o : CH * layer + o + 1, :], (8, LANES)
            )


def exchange(pieces, axis, route):
    return [pieces[0]] + [lax.ppermute(pieces[k], axis, route(k)) for k in range(1, 4)]


def shards(
    blk_temp, blk_qual, dest_tile, blk_offset, background, reflect, land,
    conv_first, bias_first, conv_second, bias_second, conv_third, bias_third, head,
):
    tile = lax.axis_index("tiles")
    s = lax.axis_index("swath")
    tiles = lax.axis_size("tiles")
    x, z, c = tile // (2 * NZ), (tile // 2) % NZ, tile % 2
    first = tile == 0
    last = tile == tiles - 1
    info = jnp.stack(
        [x, z, c, s, first, last, first & (s == 0), last & (s == NY - 1)]
    ).astype(jnp.int32)

    count = blk_temp.shape[0]
    down = [(i, i + 1) for i in range(tiles - 1)]
    up = [(i + 1, i) for i in range(tiles - 1)]

    def edge(last_rows):
        at = TR // HALO - 1 if last_rows else 0
        return [
            pl.BlockSpec((NBANDS, HALO, LANES), lambda i: (0, at, 0)),
            pl.BlockSpec((HALO, LANES), lambda i: (at, 0)),
            pl.BlockSpec((HALO, LANES), lambda i: (at, 0)),
        ]

    edges = [spec for pair in zip(edge(False), edge(True)) for spec in pair]
    row_h, row_l = band_matrix(np.arange(RQ), np.arange(RQ))
    natural = np.arange(COLS)
    place = NY * (natural % LANES) + natural // LANES
    col_h, col_l = band_matrix(natural, place)
    turn = jnp.asarray((natural[:, None] == place[None, :]).astype(bf16))
    turn_back = jnp.asarray((place[:, None] == natural[None, :]).astype(bf16))
    lanes = np.arange(2 * LANES)
    spot = np.where(lanes < LANES + HALO, lanes, lanes - LANES - 2 * HALO)
    spot = np.where(lanes < LANES + 2 * HALO, spot, 1000 * lanes)
    near_h, near_l = band_matrix(spot, spot)

    strip = sds((NBANDS + 1, STRIP, LANES), bf16)
    first_columns, last_columns = call(slab_kernel, (strip, strip), [VMEM] * 2, name="slab")(
        reflect, land
    )
    from_left = lax.ppermute(last_columns, "swath", [(i, i + 1) for i in range(NY - 1)])
    from_right = lax.ppermute(first_columns, "swath", [(i + 1, i) for i in range(NY - 1)])
    packed = call(
        pack_kernel,
        (sds((2 * count * BR + HALO, LANES), bf16),) * 4,
        [SMEM] * 3 + [VMEM] * 2,
        name="pack",
    )(info, dest_tile, blk_offset, blk_temp, blk_qual)
    block = sds(packed[0].shape, bf16)
    packed = tuple(packed[0:1]) + tuple(call(
        order_kernel, (block,) * 3, [ANY] * 5, place=ANY, alias={0: 0, 1: 1, 2: 2}, name="order"
    )(*packed[1:], from_left, from_right))
    edge_rows = sds((NBANDS + 3, HALO, 2 * LANES), bf16)
    top, bottom = call(
        edges_kernel, (edge_rows,) * 2, edges + [VMEM] * 2, grid=(1,), name="edges"
    )(reflect, reflect, land, land, background, background, from_left, from_right)
    above = lax.ppermute(bottom, "tiles", down)
    below = lax.ppermute(top, "tiles", up)

    adjoint, normal, window = call(
        adjoint_kernel,
        (
            sds((NBANDS + 1, TR, LANES), f32),
            sds((8, LANES), f32),
            sds((NBANDS + 1, WIN, LANES), bf16),
        ),
        [VMEM] * 10,
        scratch=[
            pltpu.VMEM((NBANDS + 1, WIN, LANES), bf16),
            pltpu.VMEM((NBANDS, RQ, 2 * LANES), f32),
        ],
        name="adjoint",
    )(reflect, land, above, below, from_left, from_right, row_h, row_l, near_h, near_l)
    taps = jnp.transpose(jnp.stack([conv_first, conv_second, conv_third]), (0, 3, 4, 1, 2))
    bias = jnp.concatenate([bias_first, bias_second, bias_third])
    kernels, biases = call(
        matrices_kernel,
        (sds((3, CH * 8, 3 * KROWS), bf16), sds((3, CH * 8, LANES), f32)),
        [VMEM] * 2,
        name="matrices",
    )(taps, jnp.broadcast_to(bias[:, None], (3 * CH, LANES)))
    weights = head.astype(f32)

    chip = exchange(packed, "swath", along_y)
    chip[1] = call(
        order_kernel, (block,), [ANY] * 3, place=ANY, alias={0: 0}, name="order"
    )(chip[1], adjoint, kernels)[0]
    cut = call(
        cut_kernel,
        sds((NY, NBANDS + 1, RQ, LANES), bf16),
        [VMEM] + [ANY],
        name="cut",
    )(window, chip[2])
    pieces = lax.all_to_all(cut, "swath", split_axis=0, concat_axis=0, tiled=True)
    fields, bands = call(
        bands_kernel,
        (sds((NBANDS + 1, RQ, COLS), bf16), sds((NBANDS, RQ, COLS), f32)),
        [SMEM] + [VMEM] * 6,
        scratch=[pltpu.VMEM((NBANDS + 1, RQ, COLS), bf16)],
        flops=2 * 6 * 160 * 512 * (320 + 1536),
        nbytes=10 << 20,
        name="bands",
    )(info, pieces, row_h, row_l, col_h, col_l, turn)
    chip[2] = call(
        order_kernel, (block,), [ANY] * 2, place=ANY, alias={0: 0}, name="order"
    )(chip[2], cut)[0]
    chip = chip + [lax.ppermute(p, "tiles", core_pair) for p in chip]

    part = sds((4, WIN, LANES), bf16)
    routed = call(
        scatter_kernel,
        (part,) * 8,
        [SMEM] + [ANY] * 9,
        scratch=scatter_scratch(2 * count * BR),
        place=ANY,
        flops=96 * 128 * 128 * 8,
        nbytes=12 << 20,
        name="scatter",
    )(info, *chip, cut)
    nums = exchange(routed[0:4], "tiles", along_x)
    dens = exchange(routed[4:8], "tiles", along_z)

    one = sds((WIN, LANES), f32)
    summed = call(sum_kernel, (one,) * 4, [VMEM] * 4 + [ANY], nbytes=3 << 20, name="add")
    nums = summed(*nums, fields)
    dens = summed(*dens, fields)
    nums = exchange(nums, "tiles", along_z)
    dens = exchange(dens, "tiles", along_x)
    rows = call(
        blend_kernel,
        (sds((RQ + 8, LANES), f32),) * 4,
        [SMEM] + [VMEM] * 13,
        scratch=[pltpu.VMEM((WIN, LANES), f32)],
        nbytes=3 << 20,
        name="blend",
    )(info, *nums, *dens, background, above, below, adjoint, normal)
    rows = exchange(rows, "swath", along_y)
    sums = call(
        merge_kernel,
        sds((tiles, 8, LANES), f32),
        [pl.BlockSpec((8, LANES), lambda i: (RQ // 8, 0))] * 4,
        grid=(1,),
        name="merge",
    )(*rows)
    sums = lax.all_to_all(sums, "tiles", split_axis=0, concat_axis=0, tiled=True)
    coarse, stacked = call(
        assemble_kernel,
        (sds((RQ, COLS), f32), sds((GROUPS, KROWS, 6 * LANES), bf16)),
        [SMEM] + [VMEM] * 9 + [ANY] * 2,
        scratch=assemble_scratch(),
        place=(VMEM, ANY),
        flops=2 * 160 * 512 * (480 + 1536),
        nbytes=8 << 20,
        name="assemble",
    )(info, *rows, row_h, row_l, col_h, col_l, turn, fields, bands)
    *sharp, fit_coefs = call(
        main_kernel,
        (sds((QROWS, LANES), f32),) * 4 + (sds((NBANDS + 1,), f32),),
        [SMEM, SMEM, VMEM] + [ANY] * 3 + [VMEM] * 2 + [ANY] * 2,
        scratch=main_scratch(),
        flops=3 * 18 * 2 * 384 * 160 * 512,
        nbytes=8 << 20,
        name="convolve",
    )(info, weights, sums, coarse, fields, bands, kernels, biases, turn_back, stacked)
    sharp = exchange(sharp, "swath", along_y)
    out = call(join_kernel, sds((TR, LANES), f32), [SMEM] + [VMEM] * 4, name="join")(info, *sharp)
    return out, fit_coefs


def solution(mesh):
    placed = (
        P(("tiles", "swath"), None, None),
        P(("tiles", "swath"), None, None),
        P(("tiles", "swath")),
        P(("tiles", "swath")),
        P("tiles", "swath"),
        P(None, "tiles", "swath"),
        P("tiles", "swath"),
        P(),
        P(),
        P(),
        P(),
        P(),
        P(),
        P(),
    )
    return jax.shard_map(
        shards, mesh=mesh, in_specs=placed, out_specs=(P("tiles", "swath"), P()), check_vma=False
    )
```
